256 devices in a mesh: lat: 64 (over z, y, x_lo), ch: 4 (over x_hi, core).
Axes of the slice: x: 4 (x_hi: 2, x_lo: 2; x = x_hi * 2 + x_lo), y: 4, z: 8, core: 2. Of those that a mesh axis runs over, the one named last changes fastest.
Arguments:
- output_gradient: bfloat16 [256, 900, 256], P('lat', None, 'ch'), may hold values from -6 to 6
- conv_in: bfloat16 [256, 900, 768], P('lat', None, 'ch'), may hold values from -6 to 6
- conv_weight: bfloat16 [3, 3, 768, 256], P(None, None, 'ch'), may hold values from -0.078125 to 0.078125
- modes: bfloat16 [448, 256, 8, 2, 96], P('lat', None, 'ch'), may hold values from -6 to 6
- w1: bfloat16 [8, 2, 96, 96], P('ch'), may hold values from -0.4375 to 0.4375
- b1: bfloat16 [8, 2, 96], P('ch'), may hold values from -6 to 6
- w2: bfloat16 [8, 2, 96, 96], P('ch'), may hold values from -0.4375 to 0.4375
Outputs:
- grad_in: bfloat16 [256, 900, 768], P('lat', None, 'ch')
- grad_conv: float32 [3, 3, 768, 256], P(None, None, 'ch')
- grad_w1: float32 [8, 2, 96, 96], P('ch')
- grad_b1: float32 [8, 2, 96], P('ch')
- grad_w2: float32 [8, 2, 96, 96], P('ch')
- grad_b2: float32 [8, 2, 96], P('ch')
The draws below stay inside these ranges and needn't reach their ends.
All inputs are finite; a program needn't handle non-finite values.
Results may differ from the reference program's by a relative error of at most 0.012.
Values may be sent and summed in bfloat16 or wider, within the bound.
A program may use at most 128 MiB of HBM per device.

```python
import math
import jax
import jax.numpy as jnp
from jax import lax

D = 768
NB = 8
BS = 96
CO = 256
LON = 900
KX = 448
DILATION_STEP = 4
LAT = 256


def levels(key, dims, cuts, low, top_value):
    loudness, own = 1.0, jax.random.fold_in(key, 6)
    for position, blocks in cuts:
        heights = jnp.exp(jax.random.uniform(jax.random.fold_in(own, position), (blocks,), jnp.float32, low / len(cuts), top_value / len(cuts)))
        loudness = loudness * jnp.repeat(heights, dims[position] // blocks).reshape([-1 if axis == position else 1 for axis in range(len(dims))])
    return loudness


def gaussian(own_key, shape, deviation, bound, shards=(), kind=jnp.bfloat16):
    result = jax.random.normal(own_key, shape, jnp.float32) * deviation
    if len(shards) > 0:
        result = levels(own_key, shape, shards, -0.22, 0.18) * result
    return jnp.clip(result, min=-bound, max=bound).astype(kind)


def setup_inputs(seed: int = 0) -> dict:
    splits = jax.random.split(jax.random.key(seed), 8)
    return {
        "output_gradient": gaussian(splits[0], (LAT, LON, CO), 1.0, 6.0, ((0, 64), (2, 4))),
        "conv_in": gaussian(splits[1], (LAT, LON, D), 1.0, 6.0, ((0, 64), (2, 4))),
        "conv_weight": gaussian(splits[2], (3, 3, D, CO), (9 * D) ** -0.5, 0.078125, ((2, 4),)),
        "modes": gaussian(splits[3], (KX, LAT, NB, 2, BS), 1.0, 6.0, ((0, 64), (2, 4))),
        "w1": gaussian(splits[4], (NB, 2, BS, BS), (2 * BS) ** -0.5, 0.4375, ((0, 4),)),
        "b1": gaussian(splits[5], (NB, 2, BS), 1.0, 6.0, ((0, 4),)),
        "w2": gaussian(splits[6], (NB, 2, BS, BS), (2 * BS) ** -0.5, 0.4375, ((0, 4),)),
    }


def smooth_gate(values):
    return jax.nn.gelu(values, approximate=True)

def analysis_table(lon_count, mode_count):
    positions = jnp.arange(lon_count, dtype=jnp.int32)[:, None]
    wavenums = jnp.arange(mode_count, dtype=jnp.int32)[None, :]
    angle_index = positions * wavenums % lon_count
    angles = angle_index.astype(jnp.float32) * (2.0 * math.pi / lon_count)
    weights = jnp.where(wavenums == 0, 1.0, 2.0).astype(jnp.float32) / math.sqrt(lon_count)
    return jnp.stack([weights * jnp.cos(angles), -weights * jnp.sin(angles)], axis=1).astype(jnp.bfloat16)

def synthesis_table(lon_count, mode_count):
    wavenums = jnp.arange(mode_count, dtype=jnp.int32)[:, None]
    positions = jnp.arange(lon_count, dtype=jnp.int32)[None, :]
    angle_index = positions * wavenums % lon_count
    angles = angle_index.astype(jnp.float32) * (2.0 * math.pi / lon_count)
    factor = 1.0 / math.sqrt(lon_count)
    return jnp.stack([factor * jnp.cos(angles), -factor * jnp.sin(angles)], axis=0).astype(jnp.bfloat16)

def lat_tables(lat_count):
    wavenums = jnp.arange(lat_count, dtype=jnp.int32)[:, None]
    positions = jnp.arange(lat_count, dtype=jnp.int32)[None, :]
    angle_index = wavenums * positions % lat_count
    angles = angle_index.astype(jnp.float32) * (2.0 * math.pi / lat_count)
    cosine = jnp.cos(angles) / math.sqrt(lat_count)
    sine = jnp.sin(angles) / math.sqrt(lat_count)
    forward = jnp.stack([jnp.stack([cosine, sine], axis=-1), jnp.stack([-sine, cosine], axis=-1)], axis=1)
    cos_t = cosine.T
    sin_t = sine.T
    inverse = jnp.stack([jnp.stack([cos_t, -sin_t], axis=-1), jnp.stack([sin_t, cos_t], axis=-1)], axis=1)
    return (forward.astype(jnp.bfloat16), inverse.astype(jnp.bfloat16))

def complex_matrix(weight):
    real_part = weight[:, 0]
    imag_part = weight[:, 1]
    upper = jnp.concatenate([real_part, imag_part], axis=2)
    lower = jnp.concatenate([-imag_part, real_part], axis=2)
    return jnp.concatenate([upper, lower], axis=1)

def collapse(gradient, block_size):
    upper_left = gradient[:, :block_size, :block_size]
    upper_right = gradient[:, :block_size, block_size:]
    lower_left = gradient[:, block_size:, :block_size]
    lower_right = gradient[:, block_size:, block_size:]
    return jnp.stack([upper_left + lower_right, upper_right - lower_left], axis=1)

def block_backward(mode_vals, spec_vals, w1, b1, w2):
    block_size = w1.shape[-1]
    first = complex_matrix(w1).astype(jnp.float32)
    second = complex_matrix(w2).astype(jnp.float32)
    mode_wide = mode_vals.astype(jnp.float32)
    spec_wide = spec_vals.astype(jnp.float32)
    bias = b1.reshape(b1.shape[0], 2 * block_size).astype(jnp.float32)
    pre_act = jnp.einsum('mbi,bij->mbj', mode_wide, first) + bias
    activated, slope = jax.vjp(smooth_gate, pre_act)
    act_half = activated.astype(jnp.bfloat16).astype(jnp.float32)
    d_act = jnp.einsum('mbj,bij->mbi', spec_wide, second)
    d_pre = slope(d_act)[0].astype(jnp.bfloat16)
    d_pre_wide = d_pre.astype(jnp.float32)
    d_modes = jnp.einsum('mbj,bij->mbi', d_pre_wide, first).astype(jnp.bfloat16)
    grad_second = collapse(jnp.einsum('mbi,mbj->bij', act_half, spec_wide), block_size)
    grad_first = collapse(jnp.einsum('mbi,mbj->bij', mode_wide, d_pre_wide), block_size)
    bias_second = lax.optimization_barrier(jnp.sum(spec_wide, axis=0)).reshape(-1, 2, block_size)
    bias_first = lax.optimization_barrier(jnp.sum(d_pre_wide, axis=0)).reshape(-1, 2, block_size)
    return (d_modes, grad_first, bias_first, grad_second, bias_second)

def reference(output_gradient, conv_in, conv_weight, modes, w1, b1, w2):
    padded_gradient = jnp.pad(output_gradient, ((DILATION_STEP, DILATION_STEP), (0, 0), (0, 0)))
    conv_grad = jnp.zeros((LAT, LON, D), jnp.float32)
    flat_in = conv_in.reshape(LAT * LON, D)
    kernel_terms = []
    for row_offset in range(3):
        start_offset = DILATION_STEP - DILATION_STEP * (row_offset - 1)
        window_strip = padded_gradient[start_offset:start_offset + LAT]
        for column_offset in range(3):
            shifted_window = jnp.roll(window_strip, DILATION_STEP * (column_offset - 1), axis=1)
            flat_tap = shifted_window.reshape(LAT * LON, CO)
            conv_grad = conv_grad + jnp.dot(flat_tap, conv_weight[row_offset, column_offset].T, preferred_element_type=jnp.float32).reshape(LAT, LON, D)
            kernel_terms.append(jnp.dot(flat_in.T, flat_tap, preferred_element_type=jnp.float32))
    grad_conv = jnp.stack(kernel_terms).reshape(3, 3, D, CO)
    half_grad = conv_grad.astype(jnp.bfloat16)
    lon_table = analysis_table(LON, KX)
    lon_modes = jnp.einsum('pqc,qik->pikc', half_grad.astype(jnp.float32), lon_table.astype(jnp.float32)).astype(jnp.bfloat16)
    lon_modes = lon_modes.reshape(LAT, 2, KX, NB, BS)
    lat_forward, lat_inverse = lat_tables(LAT)
    spec_grad = jnp.einsum('yopi,pikbs->kybos', lat_forward.astype(jnp.float32), lon_modes.astype(jnp.float32)).astype(jnp.bfloat16)
    spec_rows = spec_grad.reshape(KX * LAT, NB, 2 * BS)
    mode_rows = modes.reshape(KX * LAT, NB, 2 * BS)
    d_modes, grad_w1, grad_b1, grad_w2, grad_b2 = block_backward(mode_rows, spec_rows, w1, b1, w2)
    d_modes = d_modes.reshape(KX, LAT, NB, 2, BS)
    back_modes = jnp.einsum('poyi,kybis->pokbs', lat_inverse.astype(jnp.float32), d_modes.astype(jnp.float32)).astype(jnp.bfloat16)
    back_modes = back_modes.reshape(LAT, 2, KX, D)
    syn_table = synthesis_table(LON, KX)
    spectral_part = jnp.einsum('pikc,ikq->pqc', back_modes.astype(jnp.float32), syn_table.astype(jnp.float32))
    grad_in = (conv_grad + spectral_part).astype(jnp.bfloat16)
    return (grad_in, grad_conv, grad_w1, grad_b1, grad_w2, grad_b2)
```

```python
import functools
import math

import jax
import jax.numpy as jnp
import ml_dtypes
import numpy as np
from jax import lax
from jax.experimental import pallas as pl
from jax.experimental.pallas import tpu as pltpu
from jax.sharding import PartitionSpec as P

MESH = pl.DeviceIdType.MESH
F32, BF16 = jnp.float32, jnp.bfloat16
STEP = 4
LON, PAD = 900, 1024
NLAT = 64
ROWS = 4
NK = 7
KX = 448
CI, CO = 192, 256
PC = ROWS * CI
VMEM = 56 * 1024 * 1024
NT = (((1,), (1,)), ((), ()))
TN = (((0,), (0,)), ((), ()))
NN = (((1,), (0,)), ((), ()))


def dot(a, b, dims=NN):
    return lax.dot_general(a, b, dims, preferred_element_type=F32)


def lon_tables():
    q = np.arange(LON)[None, :]
    d, i, kk = np.meshgrid(np.arange(NLAT), np.arange(2), np.arange(8), indexing="ij")
    k = (d * NK + kk).reshape(-1, 1)
    i = i.reshape(-1, 1)
    live = (kk.reshape(-1, 1) < NK).astype(np.float64)
    angle = (k * q % LON) * (2.0 * math.pi / LON)
    base = np.where(i == 0, np.cos(angle), -np.sin(angle)) / math.sqrt(LON) * live
    weight = np.where(k == 0, 1.0, 2.0)
    pad = ((0, 0), (0, PAD - LON))
    ana = np.pad(base * weight, pad).astype(ml_dtypes.bfloat16)
    syn = np.pad(base, pad).astype(ml_dtypes.bfloat16)
    return ana, syn


def lat_tables():
    y = np.arange(NLAT)[:, None]
    l = np.arange(NLAT)[None, :]
    angle = (y * l % NLAT) * (2.0 * math.pi / NLAT)
    c, s = np.cos(angle) / 16.0, np.sin(angle) / 16.0
    small = np.array([[c, s], [-s, c]])
    fwd = np.zeros((NK, 2, NLAT, NLAT, 2, 8))
    for k in range(NK):
        fwd[k, :, :, :, :, k] = small.transpose(0, 2, 3, 1)
    fwd = fwd.reshape(NK, 2 * NLAT, 16 * NLAT)
    back = np.array([[c, -s], [s, c]])
    inv = np.zeros((NLAT, 2, 8, NK, 2, NLAT))
    for k in range(NK):
        inv[:, :, k, k] = back.transpose(3, 0, 1, 2)
    inv = inv.reshape(16 * NLAT, NK * 2 * NLAT)
    tw = np.zeros((2, ROWS, NLAT, 1))
    for p in range(ROWS):
        a = np.arange(NLAT) * p * (2.0 * math.pi / 256)
        tw[0, p, :, 0], tw[1, p, :, 0] = np.cos(a), np.sin(a)
    tw = np.broadcast_to(tw, (2, ROWS, NLAT, CI))
    return (
        fwd.astype(ml_dtypes.bfloat16),
        inv.astype(ml_dtypes.bfloat16),
        np.ascontiguousarray(tw).astype(np.float32),
    )


def gather_kernel(g_ref, out_ref, send, recv, local):
    me = lax.axis_index("lat")
    ch = lax.axis_index("ch")
    xlo = lax.rem(me, 2)
    near = 2 * xlo
    far = 2 - near
    pair = me + 1 - 2 * xlo
    ch2 = lax.rem(ch + 2, 4)
    core = ch + 1 - 2 * lax.rem(ch, 2)
    nxt = lax.rem(me + 2 - 4 * xlo + NLAT, NLAT)
    prv = lax.rem(me - 2 + 4 * xlo + NLAT, NLAT)

    barrier = pltpu.get_barrier_semaphore()
    for dev in ((pair, ch), (pair, ch2), (me, core), (nxt, ch), (prv, ch)):
        pl.semaphore_signal(barrier, inc=1, device_id=dev, device_id_type=MESH)
    pl.semaphore_wait(barrier, 5)

    def rows(c):
        return pl.ds(pl.multiple_of(c * 64, 64), 64)

    def at(p, slot, c):
        return out_ref.at[p, slot, rows(c), :]

    started = []

    def go(src, dst, kind, p, dev):
        copy = pltpu.make_async_remote_copy(
            src_ref=src,
            dst_ref=dst,
            send_sem=send.at[kind, p],
            recv_sem=recv.at[kind, p],
            device_id=dev,
            device_id_type=MESH,
        )
        copy.start()
        started.append(copy)

    def got(kind, p, dst):
        pltpu.make_async_remote_copy(
            src_ref=dst,
            dst_ref=dst,
            send_sem=send.at[kind, p],
            recv_sem=recv.at[kind, p],
            device_id=(me, core),
            device_id_type=MESH,
        ).wait_recv()

    own = pltpu.make_async_copy(g_ref, out_ref.at[:, 1, rows(ch), :], local)
    own.start()
    for p in range(ROWS):
        go(g_ref.at[p], at(p, far, ch), 0, p, (pair, ch))
        go(g_ref.at[p], at(p, far, ch), 1, p, (pair, ch2))
    for p in range(ROWS):
        go(g_ref.at[p], at(p, 1, ch), 5, p, (me, core))
    for p in range(ROWS):
        got(0, p, at(p, near, ch))
        go(at(p, near, ch), at(p, far, ch), 3, p, (nxt, ch))
        if p < 2:
            go(at(p, near, ch), at(p, 1, ch), 2, p, (pair, ch2))
        go(at(p, near, ch), at(p, near, ch), 6, p, (me, core))
        got(1, p, at(p, near, ch2))
        go(at(p, near, ch2), at(p, far, ch2), 4, p, (nxt, ch))
        if p >= 2:
            go(at(p, near, ch2), at(p, 1, ch2), 2, p, (pair, ch))
        go(at(p, near, ch2), at(p, near, ch2), 7, p, (me, core))
    for p in range(ROWS):
        got(2, p, at(p, 1, ch2))
        go(at(p, 1, ch2), at(p, 1, ch2), 8, p, (me, core))
        got(3, p, at(p, far, ch))
        go(at(p, far, ch), at(p, far, ch), 9, p, (me, core))
        got(4, p, at(p, far, ch2))
        go(at(p, far, ch2), at(p, far, ch2), 10, p, (me, core))
    core2 = lax.rem(core + 2, 4)
    for p in range(ROWS):
        got(5, p, at(p, 1, core))
        got(6, p, at(p, near, core))
        got(7, p, at(p, near, core2))
        got(8, p, at(p, 1, core2))
        got(9, p, at(p, far, core))
        got(10, p, at(p, far, core2))
    own.wait()
    for copy in started:
        copy.wait_send()

    @pl.when(me == 0)
    def _():
        out_ref[:, 2] = jnp.zeros((ROWS, CO, PAD), BF16)

    @pl.when(me == NLAT - 1)
    def _():
        out_ref[:, 0] = jnp.zeros((ROWS, CO, PAD), BF16)


def gather(g):
    return pl.pallas_call(
        gather_kernel,
        out_shape=jax.ShapeDtypeStruct((ROWS, 3, CO, PAD), BF16),
        in_specs=[pl.BlockSpec(memory_space=pltpu.VMEM)],
        out_specs=pl.BlockSpec(memory_space=pltpu.VMEM),
        scratch_shapes=[
            pltpu.SemaphoreType.DMA((11, ROWS)),
            pltpu.SemaphoreType.DMA((11, ROWS)),
            pltpu.SemaphoreType.DMA,
        ],
        compiler_params=pltpu.CompilerParams(
            collective_id=0, has_side_effects=True, vmem_limit_bytes=VMEM
        ),
        name="gather_rows",
    )(g)


def shifted(x, s):
    if s == 0:
        return x
    lane = lax.broadcasted_iota(jnp.int32, x.shape, 1)
    if s > 0:
        return jnp.where(lane < s, pltpu.roll(x, PAD - LON + s, 1), pltpu.roll(x, s, 1))
    return jnp.where(lane >= LON + s, pltpu.roll(x, LON + s, 1), pltpu.roll(x, PAD + s, 1))


def conv_kernel(g_ref, ci_ref, w_ref, ana_ref, cg_ref, a_ref, q_ref, hg_ref, acc_ref, cib_ref):
    acc_ref[...] = jnp.zeros_like(acc_ref)

    def row(p, carry):
        g = g_ref[p].reshape(3 * CO, PAD)
        total = jnp.zeros((CI, PAD), F32)
        for b in range(3):
            part = dot(w_ref[b * CI : (b + 1) * CI, :], g)
            total = total + shifted(part, STEP * (b - 1))
        at = pl.ds(pl.multiple_of(p * CI, CI), CI)
        cg_ref[at, :] = total
        hg_ref[at, :] = total.astype(BF16)
        x = jnp.concatenate(
            [ci_ref[p].astype(F32), jnp.zeros((CI, PAD - LON), F32)], axis=1
        )
        for b in range(3):
            cib_ref[b * CI : (b + 1) * CI, :] = shifted(x, -STEP * (b - 1)).astype(BF16)
        for m in range(3):
            acc_ref[m * CI : (m + 1) * CI, :] += dot(cib_ref[m * CI : (m + 1) * CI, :], g, NT)
        return carry

    lax.fori_loop(0, ROWS, row, 0)

    def chunk(m, carry):
        at = pl.ds(pl.multiple_of(m * 128, 128), 128)
        a_ref[at, :] = dot(ana_ref[at, :], hg_ref[...], NT).astype(BF16)
        return carry

    lax.fori_loop(0, 8, chunk, 0)
    for rr in range(4):
        for cc in range(2):
            for t in range(3):
                col = cc * 384 + t * 128
                q_ref[rr * 2 + cc, t * 144 : (t + 1) * 144, :] = acc_ref[
                    rr * 144 : (rr + 1) * 144, col : col + 128
                ].astype(BF16)


def local_call(kernel, outs, scratch, name, flops):
    def call(*args):
        n_out = len(outs)
        return pl.pallas_call(
            kernel,
            out_shape=[jax.ShapeDtypeStruct(s, t) for s, t in outs],
            in_specs=[pl.BlockSpec(memory_space=pltpu.VMEM)] * len(args),
            out_specs=[pl.BlockSpec(memory_space=pltpu.VMEM)] * n_out,
            scratch_shapes=scratch,
            compiler_params=pltpu.CompilerParams(vmem_limit_bytes=VMEM),
            cost_estimate=pl.CostEstimate(flops=flops, bytes_accessed=8 << 20, transcendentals=0),
            name=name,
        )(*args)

    return call


def greet_all(me):
    barrier = pltpu.get_barrier_semaphore()

    def hello(o, carry):
        dev = {"lat": lax.rem(me + o, NLAT)}
        pl.semaphore_signal(barrier, inc=1, device_id=dev, device_id_type=MESH)
        return carry

    lax.fori_loop(1, NLAT, hello, 0)
    pl.semaphore_wait(barrier, NLAT - 1)


def swap_copy(a_ref, r_ref, send, recv, me, o):
    to = lax.rem(me + o, NLAT)
    return pltpu.make_async_remote_copy(
        src_ref=a_ref.at[to],
        dst_ref=r_ref.at[me],
        send_sem=send.at[o],
        recv_sem=recv.at[o],
        device_id={"lat": to},
        device_id_type=MESH,
    )


def swap_start(a_ref, r_ref, send, recv, local, me):
    pltpu.make_async_copy(a_ref.at[me], r_ref.at[me], local).start()

    def go(j, carry):
        swap_copy(a_ref, r_ref, send, recv, me, j).start()
        swap_copy(a_ref, r_ref, send, recv, me, NLAT - j).start()
        return carry

    lax.fori_loop(1, NLAT // 2, go, 0)
    swap_copy(a_ref, r_ref, send, recv, me, NLAT // 2).start()


def swap_wait(a_ref, r_ref, send, recv, local, me):
    def done(o, carry):
        source = lax.rem(me - o + NLAT, NLAT)
        pltpu.make_async_remote_copy(
            src_ref=a_ref.at[lax.rem(me + o, NLAT)],
            dst_ref=r_ref.at[source],
            send_sem=send.at[o],
            recv_sem=recv.at[o],
            device_id={"lat": lax.rem(me + o, NLAT)},
            device_id_type=MESH,
        ).wait()
        return carry

    lax.fori_loop(1, NLAT, done, 0)
    pltpu.make_async_copy(a_ref.at[me], r_ref.at[me], local).wait()


def swap_kernel(a_ref, r_ref, send, recv, local):
    me = lax.axis_index("lat")
    greet_all(me)
    swap_start(a_ref, r_ref, send, recv, local, me)
    swap_wait(a_ref, r_ref, send, recv, local, me)


def swap(a):
    return pl.pallas_call(
        swap_kernel,
        out_shape=jax.ShapeDtypeStruct(a.shape, a.dtype),
        in_specs=[pl.BlockSpec(memory_space=pltpu.VMEM)],
        out_specs=pl.BlockSpec(memory_space=pltpu.VMEM),
        scratch_shapes=[
            pltpu.SemaphoreType.DMA((NLAT,)),
            pltpu.SemaphoreType.DMA((NLAT,)),
            pltpu.SemaphoreType.DMA,
        ],
        compiler_params=pltpu.CompilerParams(
            collective_id=1, has_side_effects=True, vmem_limit_bytes=VMEM
        ),
        name="swap_modes",
    )(a)


ROOT = math.sqrt(2.0 / math.pi)


def filter_kernel(
    r_ref, u_ref, fwd_ref, inv_ref, tw_ref, m1_ref, m2_ref, b1_ref, out_ref, q_ref,
    e_ref, g1_ref, g2_ref, bias_ref,
):
    g1_ref[...] = jnp.zeros_like(g1_ref)
    g2_ref[...] = jnp.zeros_like(g2_ref)
    bias_ref[...] = jnp.zeros_like(bias_ref)

    def mode(k, carry):
        z = dot(fwd_ref[k], r_ref[...])
        wr, wi = [], []
        for p in range(ROWS):
            zr = z[:NLAT, p * CI : (p + 1) * CI]
            zi = z[NLAT:, p * CI : (p + 1) * CI]
            if p > 0:
                c, s = tw_ref[0, p], tw_ref[1, p]
                zr, zi = zr * c + zi * s, zi * c - zr * s
            wr.append(zr)
            wi.append(zi)
        ar, ai = wr[0] + wr[2], wi[0] + wi[2]
        br, bi = wr[0] - wr[2], wi[0] - wi[2]
        cr, ci = wr[1] + wr[3], wi[1] + wi[3]
        dr, di = wr[1] - wr[3], wi[1] - wi[3]
        vr = jnp.concatenate([ar + cr, br + di, ar - cr, br - di], axis=0).astype(BF16)
        vi = jnp.concatenate([ai + ci, bi - dr, ai - ci, bi + dr], axis=0).astype(BF16)

        u = u_ref[k]
        pre = dot(u, m1_ref[...]) + b1_ref[...]
        sq = pre * pre
        th = jnp.tanh(ROOT * pre * (1.0 + 0.044715 * sq))
        act = (0.5 * pre * (1.0 + th)).astype(BF16)
        slope = 0.5 * (1.0 + th) + 0.5 * pre * (1.0 - th * th) * (
            ROOT * (1.0 + 3.0 * 0.044715 * sq)
        )
        d_act = dot(vr, m2_ref[0], NT) + dot(vi, m2_ref[1], NT)
        d_pre = (d_act * slope).astype(BF16)
        g2_ref[0] += dot(act, vr, TN)
        g2_ref[1] += dot(act, vi, TN)
        g1_ref[...] += dot(u, d_pre, TN)
        bias_ref[0:1, :] += jnp.sum(d_pre.astype(F32), axis=0, keepdims=True)
        bias_ref[1:2, 0:CI] += jnp.sum(vr.astype(F32), axis=0, keepdims=True)
        bias_ref[2:3, 0:CI] += jnp.sum(vi.astype(F32), axis=0, keepdims=True)
        xr = dot(d_pre, m1_ref[0:CI, :], NT).astype(BF16).astype(F32)
        xi = dot(d_pre, m1_ref[CI:, :], NT).astype(BF16).astype(F32)
        xr = [xr[j * NLAT : (j + 1) * NLAT] for j in range(4)]
        xi = [xi[j * NLAT : (j + 1) * NLAT] for j in range(4)]
        ar, ai = xr[0] + xr[2], xi[0] + xi[2]
        br, bi = xr[0] - xr[2], xi[0] - xi[2]
        cr, ci = xr[1] + xr[3], xi[1] + xi[3]
        dr, di = xr[1] - xr[3], xi[1] - xi[3]
        er = [ar + cr, br - di, ar - cr, br + di]
        ei = [ai + ci, bi + dr, ai - ci, bi - dr]
        for p in range(1, ROWS):
            c, s = tw_ref[0, p], tw_ref[1, p]
            er[p], ei[p] = er[p] * c - ei[p] * s, ei[p] * c + er[p] * s
        at = pl.multiple_of(k * 2 * NLAT, 2 * NLAT)
        e_ref[pl.ds(at, NLAT), :] = jnp.concatenate(er, axis=1).astype(BF16)
        e_ref[pl.ds(at + NLAT, NLAT), :] = jnp.concatenate(ei, axis=1).astype(BF16)
        return carry

    lax.fori_loop(0, NK, mode, 0)

    def chunk(m, carry):
        at = pl.ds(pl.multiple_of(m * 128, 128), 128)
        out_ref[at, :] = dot(inv_ref[at, :], e_ref[...]).astype(BF16)
        return carry

    lax.fori_loop(0, 8, chunk, 0)

    q_ref[...] = jnp.zeros_like(q_ref)
    g1 = g1_ref[...]
    h1 = (g1[:CI, :CI] + g1[CI:, CI:], g1[:CI, CI:] - g1[CI:, :CI])
    h2 = (g2_ref[0, :CI, :] + g2_ref[1, CI:, :], g2_ref[1, :CI, :] - g2_ref[0, CI:, :])
    bias = bias_ref[...]
    b1 = (bias[0:1, :CI], bias[0:1, CI:])
    b2 = (bias[1:2, :CI], bias[2:3, :CI])
    for w, (h, b) in enumerate(((h1, b1), (h2, b2))):
        for n in range(2):
            for part in range(2):
                j = w * 4 + n * 2 + part
                q_ref[j, 0:96, 0:96] = h[part][n * 96 : (n + 1) * 96, n * 96 : (n + 1) * 96].astype(BF16)
                tail = jnp.broadcast_to(b[part][:, n * 96 : (n + 1) * 96], (16, 96))
                q_ref[j, 96:112, 0:96] = tail.astype(BF16)


QC, QF, QR, QZ = 432, 112, 544, 80


def back_kernel(
    a_ref, qc_ref, qf_ref, r_ref, out_ref, in1, buf2, in2, buf4,
    send, recv, local, send1, recv1, send2, recv2, send3, recv3, send4, recv4, local4,
):
    me = lax.axis_index("lat")
    z, spot = me // 8, lax.rem(me, 8)
    greet_all(me)

    def plane(o):
        return z * 8 + lax.rem(spot + o, 8)

    def column(o):
        return lax.rem(z + o, 8) * 8 + spot

    def remote(src, dst, s, r, lat):
        return pltpu.make_async_remote_copy(
            src_ref=src, dst_ref=dst, send_sem=s, recv_sem=r,
            device_id={"lat": lat}, device_id_type=MESH,
        )

    def first(o, slot):
        peer = lax.rem(spot + o, 8)
        return (
            remote(qc_ref.at[peer], in1.at[slot, pl.ds(0, QC), :], send1.at[0, o], recv1.at[0, o], plane(o)),
            remote(qf_ref.at[peer], in1.at[slot, pl.ds(QC, QF), :], send1.at[1, o], recv1.at[1, o], plane(o)),
        )

    for o in range(1, 8):
        for copy in first(o, spot):
            copy.start()
    swap_start(a_ref, r_ref, send, recv, local, me)

    total_c = qc_ref[spot].astype(F32)
    total_f = qf_ref[spot].astype(F32)
    for o in range(1, 8):
        slot = lax.rem(spot - o + 8, 8)
        for copy in first(o, slot):
            copy.wait()
        total_c = total_c + in1[slot, 0:QC, :].astype(F32)
        total_f = total_f + in1[slot, QC:QR, :].astype(F32)
    buf2[0:QC, :] = total_c.astype(BF16)
    buf2[QC:QR, :] = total_f.astype(BF16)
    buf2[QR:, :] = jnp.zeros((8 * QZ - QR, 128), BF16)

    def zrows(i):
        return pl.ds(pl.multiple_of(i * QZ, 16), QZ)

    def second(o, slot):
        return remote(buf2.at[zrows(lax.rem(z + o, 8)), :], in2.at[slot], send2.at[o], recv2.at[o], column(o))

    for o in range(1, 8):
        second(o, z).start()
    total = buf2[zrows(z), :].astype(F32)
    for o in range(1, 8):
        slot = lax.rem(z - o + 8, 8)
        second(o, slot).wait()
        total = total + in2[slot].astype(F32)
    buf4[zrows(z), :] = total.astype(BF16)

    def third(o, slot):
        return remote(buf4.at[zrows(z), :], buf4.at[zrows(slot), :], send3.at[o], recv3.at[o], column(o))

    for o in range(1, 8):
        third(o, z).start()
    for o in range(1, 8):
        third(o, lax.rem(z - o + 8, 8)).wait()

    def fourth(o, slot):
        return remote(buf4.at[pl.ds(0, QR), :], out_ref.at[slot], send4.at[o], recv4.at[o], plane(o))

    own = pltpu.make_async_copy(buf4.at[pl.ds(0, QR), :], out_ref.at[spot], local4)
    own.start()
    for o in range(1, 8):
        fourth(o, spot).start()
    for o in range(1, 8):
        fourth(o, lax.rem(spot - o + 8, 8)).wait()
    own.wait()
    swap_wait(a_ref, r_ref, send, recv, local, me)


def back(a, qc, qf):
    dma = pltpu.SemaphoreType.DMA
    return pl.pallas_call(
        back_kernel,
        out_shape=[
            jax.ShapeDtypeStruct(a.shape, a.dtype),
            jax.ShapeDtypeStruct((8, QR, 128), BF16),
        ],
        in_specs=[pl.BlockSpec(memory_space=pltpu.VMEM)] * 3,
        out_specs=[pl.BlockSpec(memory_space=pltpu.VMEM)] * 2,
        scratch_shapes=[
            pltpu.VMEM((8, QR, 128), BF16),
            pltpu.VMEM((8 * QZ, 128), BF16),
            pltpu.VMEM((8, QZ, 128), BF16),
            pltpu.VMEM((8 * QZ, 128), BF16),
            dma((NLAT,)), dma((NLAT,)), dma,
            dma((2, 8)), dma((2, 8)), dma((8,)), dma((8,)),
            dma((8,)), dma((8,)), dma((8,)), dma((8,)), dma,
        ],
        compiler_params=pltpu.CompilerParams(
            collective_id=2, has_side_effects=True, vmem_limit_bytes=VMEM
        ),
        name="swap_back",
    )(a, qc, qf)


def synth_kernel(r_ref, syn_ref, cg_ref, q_ref, out_ref, gc_ref):
    for m in range(6):
        at = slice(m * 128, (m + 1) * 128)
        part = dot(r_ref[:, at], syn_ref[...], TN) + cg_ref[at, :]
        out_ref[at, :] = part[:, :LON].astype(BF16)
    for rr in range(4):
        for cc in range(2):
            for t in range(3):
                a, o = divmod(cc * 384 + t * 128, CO)
                r = rr * 144
                while r < (rr + 1) * 144:
                    b, c = divmod(r, CI)
                    n = min(CI - c, (rr + 1) * 144 - r)
                    at = t * 144 + r - rr * 144
                    gc_ref[a, b, c : c + n, o : o + 128] = q_ref[rr * 2 + cc, at : at + n, :].astype(F32)
                    r += n


def block_diag(w, part):
    zero = jnp.zeros_like(w[0, part])
    return jnp.concatenate(
        [
            jnp.concatenate([w[0, part], zero], axis=1),
            jnp.concatenate([zero, w[1, part]], axis=1),
        ],
        axis=0,
    )


def on_device(output_gradient, conv_in, conv_weight, modes, w1, b1, w2):
    ana, syn = lon_tables()
    fwd, inv, tw = lat_tables()
    g = jnp.pad(jnp.transpose(output_gradient, (0, 2, 1)), ((0, 0), (0, 0), (0, PAD - LON)))
    ci = jnp.transpose(conv_in, (0, 2, 1))
    w = jnp.transpose(conv_weight, (1, 2, 0, 3)).reshape(3 * CI, 3 * CO)
    u = jnp.transpose(modes, (0, 1, 3, 2, 4)).reshape(NK, 256, 2 * CI)
    p0, p1 = block_diag(w1, 0), block_diag(w1, 1)
    m1 = jnp.concatenate(
        [jnp.concatenate([p0, p1], axis=1), jnp.concatenate([-p1, p0], axis=1)], axis=0
    )
    p0, p1 = block_diag(w2, 0), block_diag(w2, 1)
    m2 = jnp.stack([jnp.concatenate([p0, -p1], axis=0), jnp.concatenate([p1, p0], axis=0)])
    bias = jnp.transpose(b1, (1, 0, 2)).reshape(1, 2 * CI).astype(F32)

    gathered = gather(g)
    cg, sent, qc = local_call(
        conv_kernel,
        [((PC, PAD), F32), ((16 * NLAT, PC), BF16), ((8, QC, 128), BF16)],
        [
            pltpu.VMEM((PC, PAD), BF16),
            pltpu.VMEM((3 * CI, 3 * CO), F32),
            pltpu.VMEM((3 * CI, PAD), BF16),
        ],
        "conv_terms",
        8_000_000_000,
    )(gathered, ci, w, ana)
    got = swap(sent.reshape(NLAT, 16, PC))
    sent_back, qf = local_call(
        filter_kernel,
        [((16 * NLAT, PC), BF16), ((8, QF, 128), BF16)],
        [
            pltpu.VMEM((NK * 2 * NLAT, PC), BF16),
            pltpu.VMEM((2 * CI, 2 * CI), F32),
            pltpu.VMEM((2, 2 * CI, CI), F32),
            pltpu.VMEM((8, 2 * CI), F32),
        ],
        "spectral_filter",
        6_000_000_000,
    )(got.reshape(16 * NLAT, PC), u, fwd, inv, tw, m1, m2, bias)
    own, sums = back(sent_back.reshape(NLAT, 16, PC), qc, qf)
    grad_in, grad_conv = local_call(
        synth_kernel,
        [((PC, LON), BF16), ((3, 3, CI, CO), F32)],
        [],
        "synthesis",
        1_600_000_000,
    )(own.reshape(16 * NLAT, PC), syn, cg, sums)
    grad_in = jnp.transpose(grad_in.reshape(ROWS, CI, LON), (0, 2, 1))
    small = sums[:, QC:, :96].astype(F32).reshape(2, 2, 2, QF, 96)
    grad_w, grad_b = small[:, :, :, :96], small[:, :, :, 96]
    return (grad_in, grad_conv, grad_w[0], grad_b[0], grad_w[1], grad_b[1])


def solution(mesh):
    placed = (
        P("lat", None, "ch"),
        P("lat", None, "ch"),
        P(None, None, "ch", None),
        P("lat", None, "ch", None, None),
        P("ch", None, None, None),
        P("ch", None, None),
        P("ch", None, None, None),
    )
    return jax.shard_map(
        on_device,
        mesh=mesh,
        in_specs=placed,
        out_specs=(
            P("lat", None, "ch"),
            P(None, None, "ch", None),
            P("ch", None, None, None),
            P("ch", None, None),
            P("ch", None, None, None),
            P("ch", None, None),
        ),
        check_vma=False,
    )
```

```python
import functools
import math

import jax
import jax.numpy as jnp
import ml_dtypes
import numpy as np
from jax import lax
from jax.experimental import pallas as pl
from jax.experimental.pallas import tpu as pltpu
from jax.sharding import PartitionSpec as P

MESH = pl.DeviceIdType.MESH
F32, BF16 = jnp.float32, jnp.bfloat16
STEP = 4
LON, PAD = 900, 1024
NLAT = 64
ROWS = 4
NK = 7
KX = 448
CI, CO = 192, 256
BS = 96
PS = ROWS * BS
VMEM = 56 * 1024 * 1024
NT = (((1,), (1,)), ((), ()))
TN = (((0,), (0,)), ((), ()))
NN = (((1,), (0,)), ((), ()))


def dot(a, b, dims=NN):
    return lax.dot_general(a, b, dims, preferred_element_type=F32)


def lon_tables():
    q = np.arange(LON)[None, :]
    d, i, kk = np.meshgrid(np.arange(NLAT), np.arange(2), np.arange(8), indexing="ij")
    k = (d * NK + kk).reshape(-1, 1)
    i = i.reshape(-1, 1)
    live = (kk.reshape(-1, 1) < NK).astype(np.float64)
    angle = (k * q % LON) * (2.0 * math.pi / LON)
    base = np.where(i == 0, np.cos(angle), -np.sin(angle)) / math.sqrt(LON) * live
    weight = np.where(k == 0, 1.0, 2.0)
    pad = ((0, 0), (0, PAD - LON))
    ana = np.pad(base * weight, pad).astype(ml_dtypes.bfloat16)
    syn = np.pad(base, pad).astype(ml_dtypes.bfloat16)
    return ana, syn


def lat_tables():
    y = np.arange(NLAT)[:, None]
    l = np.arange(NLAT)[None, :]
    angle = (y * l % NLAT) * (2.0 * math.pi / NLAT)
    c, s = np.cos(angle) / 16.0, np.sin(angle) / 16.0
    small = np.array([[c, s], [-s, c]])
    fwd = np.zeros((NK, 2, NLAT, NLAT, 2, 8))
    for k in range(NK):
        fwd[k, :, :, :, :, k] = small.transpose(0, 2, 3, 1)
    fwd = fwd.reshape(NK, 2 * NLAT, 16 * NLAT)
    back = np.array([[c, -s], [s, c]])
    inv = np.zeros((NLAT, 2, 8, NK, 2, NLAT))
    for k in range(NK):
        inv[:, :, k, k] = back.transpose(3, 0, 1, 2)
    inv = inv.reshape(16 * NLAT, NK * 2 * NLAT)
    tw = np.zeros((2, ROWS, NLAT, 1))
    for p in range(ROWS):
        a = np.arange(NLAT) * p * (2.0 * math.pi / 256)
        tw[0, p, :, 0], tw[1, p, :, 0] = np.cos(a), np.sin(a)
    tw = np.repeat(tw[..., 0].transpose(0, 2, 1), BS, axis=2)
    return (
        fwd.astype(ml_dtypes.bfloat16),
        inv.astype(ml_dtypes.bfloat16),
        np.ascontiguousarray(tw).astype(np.float32),
    )


def shifted(x, s):
    if s == 0:
        return x
    lane = lax.broadcasted_iota(jnp.int32, x.shape, 1)
    if s > 0:
        return jnp.where(lane < s, pltpu.roll(x, PAD - LON + s, 1), pltpu.roll(x, s, 1))
    return jnp.where(lane >= LON + s, pltpu.roll(x, LON + s, 1), pltpu.roll(x, PAD + s, 1))


class Summing:
    def __init__(self, me, parts, in1, buf2, in2, buf4, out, send, recv):
        self.z, self.spot = me // 8, lax.rem(me, 8)
        self.parts, self.in1, self.buf2, self.in2 = parts, in1, buf2, in2
        self.buf4, self.out, self.send, self.recv = buf4, out, send, recv
        self.rows, self.slot = parts.shape[1], in2.shape[1]

    def copy(self, stage, o, at):
        z, spot = self.z, self.spot
        to_spot, to_z = lax.rem(spot + o, 8), lax.rem(z + o, 8)
        if stage == 0:
            src, dst, lat = self.parts.at[to_spot], self.in1.at[at], z * 8 + to_spot
        elif stage == 1:
            src, dst, lat = self.buf2.at[self.zrows(to_z), :], self.in2.at[at], to_z * 8 + spot
        elif stage == 2:
            src, dst = self.buf4.at[self.zrows(z), :], self.buf4.at[self.zrows(at), :]
            lat = to_z * 8 + spot
        else:
            src, dst, lat = self.buf4.at[pl.ds(0, self.rows), :], self.out.at[at], z * 8 + to_spot
        return pltpu.make_async_remote_copy(
            src_ref=src,
            dst_ref=dst,
            send_sem=self.send.at[stage, o],
            recv_sem=self.recv.at[stage, o],
            device_id={"lat": lat},
            device_id_type=MESH,
        )

    def zrows(self, i):
        return pl.ds(pl.multiple_of(i * self.slot, 16), self.slot)

    def start(self, stage):
        at = self.spot if stage in (0, 3) else self.z

        def go(o, carry):
            self.copy(stage, o, at).start()
            return carry

        lax.fori_loop(1, 8, go, 0)
        if stage == 0:
            self.in1[at] = self.parts[at]
        elif stage == 1:
            self.in2[at] = self.buf2[self.zrows(at), :]
        elif stage == 3:
            self.out[at] = self.buf4[0 : self.rows, :]

    def wait(self, stage):
        at = self.spot if stage in (0, 3) else self.z

        def done(o, carry):
            self.copy(stage, o, lax.rem(at - o + 8, 8)).wait()
            return carry

        lax.fori_loop(1, 8, done, 0)
        if stage == 0:
            total = self.in1[0].astype(F32)
            for i in range(1, 8):
                total = total + self.in1[i].astype(F32)
            self.buf2[0 : self.rows, :] = total.astype(BF16)
            rest = 8 * self.slot - self.rows
            self.buf2[self.rows :, :] = jnp.zeros((rest, 128), BF16)
        elif stage == 1:
            total = self.in2[0].astype(F32)
            for i in range(1, 8):
                total = total + self.in2[i].astype(F32)
            self.buf4[self.zrows(at), :] = total.astype(BF16)


class Swap:
    def __init__(self, me, a, r, send, recv):
        self.me, self.a, self.r, self.send, self.recv = me, a, r, send, recv

    def copy(self, n, to, source):
        return pltpu.make_async_remote_copy(
            src_ref=self.a.at[n, to],
            dst_ref=self.r.at[n, source],
            send_sem=self.send.at[n, to],
            recv_sem=self.recv.at[n, source],
            device_id={"lat": to},
            device_id_type=MESH,
        )

    def start(self, n, first, count):
        def go(i, carry):
            to = first + i

            @pl.when(to != self.me)
            def _():
                self.copy(n, to, self.me).start()

            return carry

        lax.fori_loop(0, count, go, 0)

    def wait_recv(self, n):
        self.r[n, self.me] = self.a[n, self.me]

        def done(o, carry):
            other = lax.rem(self.me + o, NLAT)
            self.copy(n, other, other).wait_recv()
            return carry

        lax.fori_loop(1, NLAT, done, 0)

    def wait_send(self, n):
        def done(o, carry):
            other = lax.rem(self.me + o, NLAT)
            self.copy(n, other, other).wait_send()
            return carry

        lax.fori_loop(1, NLAT, done, 0)


ROOT = math.sqrt(2.0 / math.pi)
QC, QCZ, QF, QFZ = 432, 64, 112, 16


def fused_kernel(
    og_ref, ci_hbm, cw_hbm, u_hbm, w1_ref, b1_ref, w2_ref, tw_ref, ana_hbm, syn_hbm, fwd_hbm, inv_hbm,
    out_ref, sumc_ref, sumf_ref,
    g_ref, ci_ref, w_ref, u_ref, ana_ref, syn_ref, fwd_ref, inv_ref, m1_ref, m2_ref,
    cg_ref, hg_ref, acc_ref, cib_ref, a_ref, r_ref, b_ref, r2_ref, z_ref, e_ref,
    g1_ref, g2_ref, bias_ref, part_ref,
    qc_ref, qf_ref, c1_ref, c2_ref, c3_ref, c4_ref, f1_ref, f2_ref, f3_ref, f4_ref,
    loads, wloads, gsend, grecv, asend, arecv, bsend, brecv, csend, crecv, fsend, frecv,
):
    me = lax.axis_index("lat")
    ch = lax.axis_index("ch")
    zed = me // 8
    xlo = lax.rem(me, 2)
    near = 2 * xlo
    far = 2 - near
    pair = me + 1 - 2 * xlo
    ch2 = lax.rem(ch + 2, 4)
    core = ch + 1 - 2 * lax.rem(ch, 2)
    core2 = lax.rem(core + 2, 4)
    nxt = lax.rem(me + 2 - 4 * xlo + NLAT, NLAT)

    barrier = pltpu.get_barrier_semaphore()

    def hello(o, carry):
        dev = (lax.rem(me + o, NLAT), ch)
        pl.semaphore_signal(barrier, inc=1, device_id=dev, device_id_type=MESH)
        return carry

    for dev in ((me, core), (pair, ch2)):
        pl.semaphore_signal(barrier, inc=1, device_id=dev, device_id_type=MESH)
    lax.fori_loop(1, NLAT, hello, 0)

    def load(i):
        pairs = (
            (ci_hbm, ci_ref), (u_hbm, u_ref), (ana_hbm, ana_ref),
            (fwd_hbm, fwd_ref), (inv_hbm, inv_ref), (syn_hbm, syn_ref),
        )
        return pltpu.make_async_copy(pairs[i][0], pairs[i][1], loads.at[i])

    wcopies = []
    for a in range(3):
        for b in range(3):
            wcopies.append(
                pltpu.make_async_copy(
                    cw_hbm.at[a, b],
                    w_ref.at[pl.ds(b * CI, CI), pl.ds(a * CO, CO)],
                    wloads.at[a * 3 + b],
                )
            )
    for copy in wcopies:
        copy.start()
    for i in range(6):
        load(i).start()

    def rows(c):
        return pl.ds(pl.multiple_of(c * 64, 64), 64)

    def at(p, slot, c):
        return g_ref.at[p, slot, rows(c), :]

    blank = jnp.zeros((64, PAD - LON), F32)
    for p in range(ROWS):
        g_ref[p, 1, rows(ch), :] = jnp.concatenate(
            [og_ref[p].astype(F32), blank], axis=1
        ).astype(BF16)
    pl.semaphore_wait(barrier, NLAT + 1)

    started = []

    def hop(src, dst, kind, p, dev):
        return pltpu.make_async_remote_copy(
            src_ref=src,
            dst_ref=dst,
            send_sem=gsend.at[kind, p],
            recv_sem=grecv.at[kind, p],
            device_id=dev,
            device_id_type=MESH,
        )

    def go(src, dst, kind, p, dev):
        copy = hop(src, dst, kind, p, dev)
        copy.start()

    def got(kind, p, dst):
        hop(dst, dst, kind, p, (me, core)).wait_recv()

    for p in range(ROWS):
        go(at(p, 1, ch), at(p, far, ch), 0, p, (pair, ch))
        go(at(p, 1, ch), at(p, far, ch), 1, p, (pair, ch2))
    for p in range(ROWS):
        go(at(p, 1, ch), at(p, 1, ch), 5, p, (me, core))

    for w, m_ref in ((w1_ref, m1_ref), (w2_ref, m2_ref)):
        for n in range(2):
            re, im = w[n, 0], w[n, 1]
            m_ref[n, 0:BS, :] = jnp.concatenate([re, im], axis=1)
            m_ref[n, BS:, :] = jnp.concatenate([-im, re], axis=1)
    for copy in wcopies:
        copy.wait()

    @pl.when(me == 0)
    def _():
        w_ref[:, 2 * CO :] = jnp.zeros((3 * CI, CO), BF16)

    @pl.when(me == NLAT - 1)
    def _():
        w_ref[:, :CO] = jnp.zeros((3 * CI, CO), BF16)

    for p in range(ROWS):
        got(0, p, at(p, near, ch))
        go(at(p, near, ch), at(p, far, ch), 3, p, (nxt, ch))
        if p < 2:
            go(at(p, near, ch), at(p, 1, ch), 2, p, (pair, ch2))
        got(1, p, at(p, near, ch2))
        go(at(p, near, ch2), at(p, far, ch2), 4, p, (nxt, ch))
        if p >= 2:
            go(at(p, near, ch2), at(p, 1, ch2), 2, p, (pair, ch))
        go(at(p, near, ch), at(p, near, ch), 6, p, (me, core))
        go(at(p, near, ch2), at(p, near, ch2), 7, p, (me, core))

    def conv_row(p, carry):
        got(2, p, at(p, 1, ch2))
        go(at(p, 1, ch2), at(p, 1, ch2), 8, p, (me, core))
        got(3, p, at(p, far, ch))
        go(at(p, far, ch), at(p, far, ch), 9, p, (me, core))
        got(4, p, at(p, far, ch2))
        go(at(p, far, ch2), at(p, far, ch2), 10, p, (me, core))
        got(5, p, at(p, 1, core))
        got(6, p, at(p, near, core))
        got(7, p, at(p, near, core2))
        got(8, p, at(p, 1, core2))
        got(9, p, at(p, far, core))
        got(10, p, at(p, far, core2))
        g = g_ref[p].reshape(3 * CO, PAD)
        for b in range(3):
            part_ref[b] = dot(w_ref[b * CI : (b + 1) * CI, :], g)
        total = part_ref[1]
        for b in (0, 2):
            total = total + shifted(part_ref[b], STEP * (b - 1))
        where = pl.ds(pl.multiple_of(p * BS, 16), BS)
        for n in range(2):
            cg_ref[n, where, :] = total[n * BS : (n + 1) * BS]
            hg_ref[n, where, :] = total[n * BS : (n + 1) * BS].astype(BF16)
        return carry

    lax.fori_loop(0, ROWS, conv_row, 0)

    there = Swap(me, a_ref, r_ref, asend, arecv)
    load(2).wait()

    def analyse(t, carry):
        n = t // 4
        c = lax.rem(zed // 2 + 2 + t, 4)
        where = pl.ds(pl.multiple_of(c * 256, 256), 256)
        block = dot(ana_ref[where, :], hg_ref[n], NT).astype(BF16)
        a_ref[n, pl.ds(c * 16, 16)] = block.reshape(16, 16, PS)
        there.start(n, c * 16, 16)
        return carry

    lax.fori_loop(0, 8, analyse, 0)

    load(0).wait()
    acc_ref[...] = jnp.zeros_like(acc_ref)
    blank2 = jnp.zeros((CI, PAD - LON), F32)

    def kernel_row(p, carry):
        g = g_ref[p].reshape(3 * CO, PAD)
        x = jnp.concatenate([ci_ref[p].astype(F32), blank2], axis=1)
        for b in range(3):
            cib_ref[b * CI : (b + 1) * CI, :] = shifted(x, -STEP * (b - 1)).astype(BF16)
        for b in range(3):
            acc_ref[b * CI : (b + 1) * CI, :] += dot(cib_ref[b * CI : (b + 1) * CI, :], g, NT)
        return carry

    lax.fori_loop(0, ROWS, kernel_row, 0)

    @pl.when(me == 0)
    def _():
        acc_ref[:, 2 * CO :] = jnp.zeros((3 * CI, CO), F32)

    @pl.when(me == NLAT - 1)
    def _():
        acc_ref[:, :CO] = jnp.zeros((3 * CI, CO), F32)

    for rr in range(4):
        for cc in range(2):
            for t in range(3):
                col = cc * 384 + t * 128
                qc_ref[rr * 2 + cc, t * 144 : (t + 1) * 144, :] = acc_ref[
                    rr * 144 : (rr + 1) * 144, col : col + 128
                ].astype(BF16)
    sumc = Summing(me, qc_ref, c1_ref, c2_ref, c3_ref, c4_ref, sumc_ref, csend, crecv)
    sumf = Summing(me, qf_ref, f1_ref, f2_ref, f3_ref, f4_ref, sumf_ref, fsend, frecv)
    sumc.start(0)

    home = Swap(me, b_ref, r2_ref, bsend, brecv)
    load(1).wait()
    load(3).wait()
    load(4).wait()
    qf_ref[...] = jnp.zeros_like(qf_ref)

    def block_filter(n, carry):
        there.wait_recv(n)
        g1_ref[...] = jnp.zeros_like(g1_ref)
        g2_ref[...] = jnp.zeros_like(g2_ref)
        bias_ref[...] = jnp.zeros_like(bias_ref)
        for half in range(2):
            at_k = slice(half * 448, (half + 1) * 448)
            z_ref[at_k, :] = dot(fwd_ref[at_k, :], r_ref[n].reshape(16 * NLAT, PS))
        b1 = b1_ref[n].astype(F32)
        b1 = jnp.concatenate([b1[0:1], b1[1:2]], axis=1)

        def mode(k, carry2):
            top = pl.multiple_of(k * 2 * NLAT, 2 * NLAT)
            zr, zi = z_ref[pl.ds(top, NLAT), :], z_ref[pl.ds(top + NLAT, NLAT), :]
            c, s = tw_ref[0], tw_ref[1]
            zr, zi = zr * c + zi * s, zi * c - zr * s
            wr = [zr[:, p * BS : (p + 1) * BS] for p in range(ROWS)]
            wi = [zi[:, p * BS : (p + 1) * BS] for p in range(ROWS)]
            ar, ai = wr[0] + wr[2], wi[0] + wi[2]
            br, bi = wr[0] - wr[2], wi[0] - wi[2]
            cr, ci = wr[1] + wr[3], wi[1] + wi[3]
            dr, di = wr[1] - wr[3], wi[1] - wi[3]
            vr = jnp.concatenate([ar + cr, br + di, ar - cr, br - di], axis=0)
            vi = jnp.concatenate([ai + ci, bi - dr, ai - ci, bi + dr], axis=0)
            v = jnp.concatenate([vr, vi], axis=1).astype(BF16)

            u = u_ref[k, n]
            pre = dot(u, m1_ref[n], TN) + b1
            sq = pre * pre
            th = jnp.tanh(ROOT * pre * (1.0 + 0.044715 * sq))
            act = (0.5 * pre * (1.0 + th)).astype(BF16)
            slope = 0.5 * (1.0 + th) + 0.5 * pre * (1.0 - th * th) * (
                ROOT * (1.0 + 3.0 * 0.044715 * sq)
            )
            d_pre = (dot(v, m2_ref[n], NT) * slope).astype(BF16)
            g2_ref[...] += dot(act, v, TN)
            g1_ref[...] += dot(u, d_pre)
            bias_ref[0:1, :] += jnp.sum(d_pre.astype(F32), axis=0, keepdims=True)
            bias_ref[1:2, :] += jnp.sum(v.astype(F32), axis=0, keepdims=True)
            x = dot(d_pre, m1_ref[n], NT).astype(BF16).astype(F32)
            xr = [x[j * NLAT : (j + 1) * NLAT, :BS] for j in range(4)]
            xi = [x[j * NLAT : (j + 1) * NLAT, BS:] for j in range(4)]
            ar, ai = xr[0] + xr[2], xi[0] + xi[2]
            br, bi = xr[0] - xr[2], xi[0] - xi[2]
            cr, ci = xr[1] + xr[3], xi[1] + xi[3]
            dr, di = xr[1] - xr[3], xi[1] - xi[3]
            er = jnp.concatenate([ar + cr, br - di, ar - cr, br + di], axis=1)
            ei = jnp.concatenate([ai + ci, bi + dr, ai - ci, bi - dr], axis=1)
            e_ref[pl.ds(top, NLAT), :] = (er * c - ei * s).astype(BF16)
            e_ref[pl.ds(top + NLAT, NLAT), :] = (ei * c + er * s).astype(BF16)
            return carry2

        lax.fori_loop(0, NK, mode, 0)
        for w, (grad, row) in enumerate(((g1_ref, 0), (g2_ref, 1))):
            full = grad[...]
            halves = (full[:BS, :BS] + full[BS:, BS:], full[:BS, BS:] - full[BS:, :BS])
            for part in range(2):
                j = w * 4 + n * 2 + part
                qf_ref[j, 0:BS, 0:BS] = halves[part].astype(BF16)
                tail = bias_ref[row : row + 1, part * BS : (part + 1) * BS]
                qf_ref[j, BS:QF, 0:BS] = jnp.broadcast_to(tail, (QF - BS, BS)).astype(BF16)

        @pl.when(n == 1)
        def _():
            sumf.start(0)

        def inverse(j, carry2):
            c = lax.rem(zed // 2 + 2 + j, 4)
            where = pl.ds(pl.multiple_of(c * 256, 256), 256)
            block = dot(inv_ref[where, :], e_ref[...]).astype(BF16)
            b_ref[n, pl.ds(c * 16, 16)] = block.reshape(16, 16, PS)
            home.start(n, c * 16, 16)
            return carry2

        lax.fori_loop(0, 4, inverse, 0)

        @pl.when(n == 0)
        def _():
            sumc.wait(0)
            sumc.start(1)

        return carry

    lax.fori_loop(0, 2, block_filter, 0)
    sumc.wait(1)
    sumc.start(2)
    sumf.wait(0)
    sumf.start(1)
    sumc.wait(2)
    sumc.start(3)
    load(5).wait()

    def synthesis(n):
        home.wait_recv(n)
        for m in range(3):
            lanes = slice(m * 128, (m + 1) * 128)
            modes = r2_ref[n].reshape(16 * NLAT, PS)[:, lanes]
            part = (dot(modes, syn_ref[...], TN) + cg_ref[n, lanes, :])[:, :LON].astype(BF16)
            r = 0
            while r < 128:
                p, s = divmod(m * 128 + r, BS)
                size = min(BS - s, 128 - r)
                out_ref[p, n * BS + s : n * BS + s + size, :] = part[r : r + size]
                r += size

    synthesis(0)
    sumf.wait(1)
    sumf.start(2)
    sumf.wait(2)
    sumf.start(3)
    synthesis(1)
    sumc.wait(3)
    sumf.wait(3)
    for n in range(2):
        there.wait_send(n)
        home.wait_send(n)

    def gather_sent(p, carry):
        for kind in range(11):
            hop(at(p, 1, ch), at(p, 1, ch), kind, p, (me, core)).wait_send()
        return carry

    lax.fori_loop(0, ROWS, gather_sent, 0)


def fused(*args):
    vmem, anywhere = pl.BlockSpec(memory_space=pltpu.VMEM), pl.BlockSpec(memory_space=pl.ANY)
    dma = pltpu.SemaphoreType.DMA
    half, wide = BF16, F32
    scratch = [
        ((ROWS, 3, CO, PAD), half), ((ROWS, CI, LON), half), ((3 * CI, 3 * CO), half),
        ((NK, 2, CI, 256), half), ((16 * NLAT, PAD), half), ((16 * NLAT, PAD), half),
        ((NK * 2 * NLAT, 16 * NLAT), half), ((16 * NLAT, NK * 2 * NLAT), half),
        ((2, CI, CI), half), ((2, CI, CI), half),
        ((2, PS, PAD), wide), ((2, PS, PAD), half), ((3 * CI, 3 * CO), wide), ((3 * CI, PAD), half),
        ((2, NLAT, 16, PS), half), ((2, NLAT, 16, PS), half), ((2, NLAT, 16, PS), half),
        ((2, NLAT, 16, PS), half), ((NK * 2 * NLAT, PS), wide), ((NK * 2 * NLAT, PS), half),
        ((CI, CI), wide), ((CI, CI), wide), ((8, CI), wide), ((3, CI, PAD), wide),
        ((8, QC, 128), half), ((8, QF, 128), half),
        ((8, QC, 128), half), ((8 * QCZ, 128), half), ((8, QCZ, 128), half), ((8 * QCZ, 128), half),
        ((8, QF, 128), half), ((8 * QFZ, 128), half), ((8, QFZ, 128), half), ((8 * QFZ, 128), half),
    ]
    return pl.pallas_call(
        fused_kernel,
        out_shape=[
            jax.ShapeDtypeStruct((ROWS, CI, LON), BF16),
            jax.ShapeDtypeStruct((8, QC, 128), BF16),
            jax.ShapeDtypeStruct((8, QF, 128), BF16),
        ],
        in_specs=[vmem] + [anywhere] * 3 + [vmem] * 4 + [anywhere] * 4,
        out_specs=[vmem] * 3,
        scratch_shapes=[pltpu.VMEM(s, t) for s, t in scratch]
        + [
            dma((6,)), dma((9,)), dma((11, ROWS)), dma((11, ROWS)),
            dma((2, NLAT)), dma((2, NLAT)), dma((2, NLAT)), dma((2, NLAT)),
            dma((4, 8)), dma((4, 8)), dma((4, 8)), dma((4, 8)),
        ],
        compiler_params=pltpu.CompilerParams(
            collective_id=0, has_side_effects=True, vmem_limit_bytes=VMEM
        ),
        cost_estimate=pl.CostEstimate(flops=16_000_000_000, bytes_accessed=32 << 20, transcendentals=0),
        name="block_backward",
    )(*args)


def unpack_kernel(c_ref, f_ref, gc_ref, w1_ref, b1_ref, w2_ref, b2_ref):
    for rr in range(4):
        for cc in range(2):
            for t in range(3):
                a, o = divmod(cc * 384 + t * 128, CO)
                r = rr * 144
                while r < (rr + 1) * 144:
                    b, c = divmod(r, CI)
                    n = min(CI - c, (rr + 1) * 144 - r)
                    at = t * 144 + r - rr * 144
                    gc_ref[a, b, c : c + n, o : o + 128] = c_ref[rr * 2 + cc, at : at + n, :].astype(F32)
                    r += n
    for w, (w_ref, b_ref) in enumerate(((w1_ref, b1_ref), (w2_ref, b2_ref))):
        for n in range(2):
            for part in range(2):
                block = f_ref[w * 4 + n * 2 + part].astype(F32)
                w_ref[n, part] = block[:BS, :BS]
                b_ref[n, part : part + 1, :] = block[BS : BS + 1, :BS]


def unpack(sumc, sumf):
    vmem = pl.BlockSpec(memory_space=pltpu.VMEM)
    outs = [(3, 3, CI, CO), (2, 2, BS, BS), (2, 2, BS), (2, 2, BS, BS), (2, 2, BS)]
    return pl.pallas_call(
        unpack_kernel,
        out_shape=[jax.ShapeDtypeStruct(s, F32) for s in outs],
        in_specs=[vmem] * 2,
        out_specs=[vmem] * 5,
        compiler_params=pltpu.CompilerParams(vmem_limit_bytes=VMEM),
        name="lay_out",
    )(sumc, sumf)


def on_device(output_gradient, conv_in, conv_weight, modes, w1, b1, w2):
    ana, syn = lon_tables()
    fwd, inv, tw = lat_tables()
    fwd = fwd.reshape(NK * 2 * NLAT, 16 * NLAT)
    grad_in, sumc, sumf = fused(
        jnp.transpose(output_gradient, (0, 2, 1)),
        jnp.transpose(conv_in, (0, 2, 1)),
        conv_weight,
        jnp.transpose(modes, (0, 2, 3, 4, 1)).reshape(NK, 2, CI, 256),
        w1, b1, w2, tw, ana, syn, fwd, inv,
    )
    grad_in = jnp.transpose(grad_in, (0, 2, 1))
    return (grad_in, *unpack(sumc, sumf))


def solution(mesh):
    placed = (
        P("lat", None, "ch"),
        P("lat", None, "ch"),
        P(None, None, "ch", None),
        P("lat", None, "ch", None, None),
        P("ch", None, None, None),
        P("ch", None, None),
        P("ch", None, None, None),
    )
    return jax.shard_map(
        on_device,
        mesh=mesh,
        in_specs=placed,
        out_specs=(
            P("lat", None, "ch"),
            P(None, None, "ch", None),
            P("ch", None, None, None),
            P("ch", None, None),
            P("ch", None, None, None),
            P("ch", None, None),
        ),
        check_vma=False,
    )
```

```python
import functools
import math

import jax
import jax.numpy as jnp
import ml_dtypes
import numpy as np
from jax import lax
from jax.experimental import pallas as pl
from jax.experimental.pallas import tpu as pltpu
from jax.sharding import PartitionSpec as P

MESH = pl.DeviceIdType.MESH
F32, BF16 = jnp.float32, jnp.bfloat16
STEP = 4
LON, PAD = 900, 1024
NLAT = 64
ROWS = 4
NK = 7
KX = 448
CI, CO = 192, 256
BS = 96
PS = ROWS * BS
VMEM = 56 * 1024 * 1024
NT = (((1,), (1,)), ((), ()))
TN = (((0,), (0,)), ((), ()))
NN = (((1,), (0,)), ((), ()))


def dot(a, b, dims=NN):
    return lax.dot_general(a, b, dims, preferred_element_type=F32)


def lon_tables():
    q = np.arange(LON)[None, :]
    d, i, kk = np.meshgrid(np.arange(NLAT), np.arange(2), np.arange(8), indexing="ij")
    k = (d * NK + kk).reshape(-1, 1)
    i = i.reshape(-1, 1)
    live = (kk.reshape(-1, 1) < NK).astype(np.float64)
    angle = (k * q % LON) * (2.0 * math.pi / LON)
    base = np.where(i == 0, np.cos(angle), -np.sin(angle)) / math.sqrt(LON) * live
    weight = np.where(k == 0, 1.0, 2.0)
    pad = ((0, 0), (0, PAD - LON))
    ana = np.pad(base * weight, pad).astype(ml_dtypes.bfloat16)
    syn = np.pad(base, pad).astype(ml_dtypes.bfloat16)
    return ana, syn


def lat_tables():
    y = np.arange(NLAT)[:, None]
    l = np.arange(NLAT)[None, :]
    angle = (y * l % NLAT) * (2.0 * math.pi / NLAT)
    c, s = np.cos(angle) / 16.0, np.sin(angle) / 16.0
    small = np.array([[c, s], [-s, c]])
    fwd = np.zeros((NK, 2, NLAT, NLAT, 2, 8))
    for k in range(NK):
        fwd[k, :, :, :, :, k] = small.transpose(0, 2, 3, 1)
    fwd = fwd.reshape(NK, 2 * NLAT, 16 * NLAT)
    back = np.array([[c, -s], [s, c]])
    inv = np.zeros((NLAT, 2, 8, NK, 2, NLAT))
    for k in range(NK):
        inv[:, :, k, k] = back.transpose(3, 0, 1, 2)
    inv = inv.reshape(16 * NLAT, NK * 2 * NLAT)
    tw = np.zeros((2, ROWS, NLAT, 1))
    for p in range(ROWS):
        a = np.arange(NLAT) * p * (2.0 * math.pi / 256)
        tw[0, p, :, 0], tw[1, p, :, 0] = np.cos(a), np.sin(a)
    tw = np.repeat(tw[..., 0].transpose(0, 2, 1), BS, axis=2)
    return (
        fwd.astype(ml_dtypes.bfloat16),
        inv.astype(ml_dtypes.bfloat16),
        np.ascontiguousarray(tw).astype(np.float32),
    )


def shifted(x, s):
    if s == 0:
        return x
    lane = lax.broadcasted_iota(jnp.int32, x.shape, 1)
    if s > 0:
        return jnp.where(lane < s, pltpu.roll(x, PAD - LON + s, 1), pltpu.roll(x, s, 1))
    return jnp.where(lane >= LON + s, pltpu.roll(x, LON + s, 1), pltpu.roll(x, PAD + s, 1))


class Summing:
    def __init__(self, me, parts, in1, buf2, in2, buf4, out, send, recv):
        self.z, self.spot = me // 8, lax.rem(me, 8)
        self.parts, self.in1, self.buf2, self.in2 = parts, in1, buf2, in2
        self.buf4, self.out, self.send, self.recv = buf4, out, send, recv
        self.rows, self.slot = parts.shape[1], in2.shape[1]

    def copy(self, stage, o, at):
        z, spot = self.z, self.spot
        to_spot, to_z = lax.rem(spot + o, 8), lax.rem(z + o, 8)
        if stage == 0:
            src, dst, lat = self.parts.at[to_spot], self.in1.at[at], z * 8 + to_spot
        elif stage == 1:
            src, dst, lat = self.buf2.at[self.zrows(to_z), :], self.in2.at[at], to_z * 8 + spot
        elif stage == 2:
            src, dst = self.buf4.at[self.zrows(z), :], self.buf4.at[self.zrows(at), :]
            lat = to_z * 8 + spot
        else:
            src, dst, lat = self.buf4.at[pl.ds(0, self.rows), :], self.out.at[at], z * 8 + to_spot
        return pltpu.make_async_remote_copy(
            src_ref=src,
            dst_ref=dst,
            send_sem=self.send.at[stage, o],
            recv_sem=self.recv.at[stage, o],
            device_id={"lat": lat},
            device_id_type=MESH,
        )

    def zrows(self, i):
        return pl.ds(pl.multiple_of(i * self.slot, 16), self.slot)

    def start(self, stage):
        at = self.spot if stage in (0, 3) else self.z

        def go(o, carry):
            self.copy(stage, o, at).start()
            return carry

        lax.fori_loop(1, 8, go, 0)
        if stage == 0:
            self.in1[at] = self.parts[at]
        elif stage == 1:
            self.in2[at] = self.buf2[self.zrows(at), :]
        elif stage == 3:
            self.out[at] = self.buf4[0 : self.rows, :]

    def wait(self, stage):
        at = self.spot if stage in (0, 3) else self.z

        def done(o, carry):
            self.copy(stage, o, lax.rem(at - o + 8, 8)).wait()
            return carry

        lax.fori_loop(1, 8, done, 0)
        if stage == 0:
            total = self.in1[0].astype(F32)
            for i in range(1, 8):
                total = total + self.in1[i].astype(F32)
            self.buf2[0 : self.rows, :] = total.astype(BF16)
            rest = 8 * self.slot - self.rows
            self.buf2[self.rows :, :] = jnp.zeros((rest, 128), BF16)
        elif stage == 1:
            total = self.in2[0].astype(F32)
            for i in range(1, 8):
                total = total + self.in2[i].astype(F32)
            self.buf4[self.zrows(at), :] = total.astype(BF16)


class Swap:
    def __init__(self, me, a, r, send, recv):
        self.me, self.a, self.r, self.send, self.recv = me, a, r, send, recv

    def copy(self, n, to, source):
        return pltpu.make_async_remote_copy(
            src_ref=self.a.at[n, to],
            dst_ref=self.r.at[n, source],
            send_sem=self.send.at[n, to],
            recv_sem=self.recv.at[n, source],
            device_id={"lat": to},
            device_id_type=MESH,
        )

    def start(self, n, z):
        def go(i, carry):
            to = z * 8 + i

            @pl.when(to != self.me)
            def _():
                self.copy(n, to, self.me).start()

            return carry

        lax.fori_loop(0, 8, go, 0)

    def wait_recv(self, n):
        self.r[n, self.me] = self.a[n, self.me]

        def done(o, carry):
            other = lax.rem(self.me + o, NLAT)
            self.copy(n, other, other).wait_recv()
            return carry

        lax.fori_loop(1, NLAT, done, 0)

    def wait_send(self, n):
        def done(o, carry):
            other = lax.rem(self.me + o, NLAT)
            self.copy(n, other, other).wait_send()
            return carry

        lax.fori_loop(1, NLAT, done, 0)


ROOT = math.sqrt(2.0 / math.pi)
QC, QCZ, QF, QFZ = 432, 64, 112, 16
LAST = ROWS - 1


def fused_kernel(
    og_ref, ci_hbm, cw_hbm, u_hbm, w1_ref, b1_ref, w2_ref, tw_ref, ana_hbm, syn_hbm, fwd_hbm, inv_hbm,
    out_ref, sumc_ref, sumf_ref,
    g_ref, ci_ref, w_ref, u_ref, ana_ref, syn_ref, fwd_ref, inv_ref, m1_ref, m2_ref,
    cg_ref, hg_ref, acc_ref, cib_ref, a_ref, r_ref, b_ref, r2_ref, z_ref, e_ref,
    g1_ref, g2_ref, bias_ref, part_ref, relay_ref, act_ref, slope_ref, v_ref, d_ref, x_ref,
    qc_ref, qf_ref, c1_ref, c2_ref, c3_ref, c4_ref, f1_ref, f2_ref, f3_ref, f4_ref,
    ready, loads, wloads, uloads, gsend, grecv, asend, arecv, bsend, brecv, csend, crecv, fsend, frecv,
):
    me = lax.axis_index("lat")
    ch = lax.axis_index("ch")
    zed = me // 8
    xlo = lax.rem(me, 2)
    near = 2 * xlo
    far = 2 - near
    pair = me + 1 - 2 * xlo
    ch2 = lax.rem(ch + 2, 4)
    core = ch + 1 - 2 * lax.rem(ch, 2)
    core2 = lax.rem(core + 2, 4)
    nxt = lax.rem(me + 2 - 4 * xlo + NLAT, NLAT)
    prv = lax.rem(me - 2 + 4 * xlo + NLAT, NLAT)

    barrier = pltpu.get_barrier_semaphore()

    spot = lax.rem(me, 8)
    for dev in ((pair, ch), (pair, ch2), (me, core), (nxt, ch), (prv, ch)):
        pl.semaphore_signal(barrier, inc=1, device_id=dev, device_id_type=MESH)

    def hello(o, carry):
        for lat in (zed * 8 + lax.rem(spot + o, 8), lax.rem(zed + o, 8) * 8 + spot):
            pl.semaphore_signal(barrier, inc=1, device_id=(lat, ch), device_id_type=MESH)
        return carry

    lax.fori_loop(1, 8, hello, 0)

    def load(i):
        pairs = (
            (ci_hbm, ci_ref), (ana_hbm, ana_ref),
            (fwd_hbm, fwd_ref), (inv_hbm, inv_ref), (syn_hbm, syn_ref),
        )
        return pltpu.make_async_copy(pairs[i][0], pairs[i][1], loads.at[i])

    wcopies = []
    for a in range(3):
        for b in range(3):
            wcopies.append(
                pltpu.make_async_copy(
                    cw_hbm.at[a, b],
                    w_ref.at[pl.ds(b * CI, CI), pl.ds(a * CO, CO)],
                    wloads.at[a * 3 + b],
                )
            )
    for copy in wcopies:
        copy.start()
    ucopies = []
    for n in range(2):
        for k in range(NK):
            ucopies.append(
                pltpu.make_async_copy(
                    u_hbm.at[k, n], u_ref.at[n, :, pl.ds(k * 256, 256)], uloads.at[n * NK + k]
                )
            )
    for copy in ucopies:
        copy.start()
    for i in range(5):
        load(i).start()

    def rows(c):
        return pl.ds(pl.multiple_of(c * 64, 64), 64)

    def at(p, slot, c):
        return g_ref.at[p, slot, rows(c), :]

    blank = jnp.zeros((64, PAD - LON), F32)
    for p in range(ROWS):
        g_ref[p, 1, rows(ch), :] = jnp.concatenate(
            [og_ref[p].astype(F32), blank], axis=1
        ).astype(BF16)
    pl.semaphore_wait(barrier, 5 + 14)

    def plane_here(o, carry):
        lat = lax.rem(zed + o, 8) * 8 + spot
        pl.semaphore_signal(ready, inc=1, device_id=(lat, ch), device_id_type=MESH)
        return carry


    started = []

    def hop(src, dst, kind, p, dev):
        return pltpu.make_async_remote_copy(
            src_ref=src,
            dst_ref=dst,
            send_sem=gsend.at[kind, p],
            recv_sem=grecv.at[kind, p],
            device_id=dev,
            device_id_type=MESH,
        )

    def go(src, dst, kind, p, dev):
        copy = hop(src, dst, kind, p, dev)
        copy.start()

    def got(kind, p, dst):
        hop(dst, dst, kind, p, (me, core)).wait_recv()

    for p in range(ROWS):
        go(at(p, 1, ch), at(p, far, ch), 0, p, (pair, ch))
        go(at(p, 1, ch), at(p, far, ch), 1, p, (pair, ch2))
        if p == 0:
            go(at(LAST, 1, ch), relay_ref, 11, LAST, (prv, ch))
    for p in range(ROWS):
        go(at(p, 1, ch), at(p, 1, ch), 5, p, (me, core))

    lax.fori_loop(1, 8, plane_here, 0)

    for w, m_ref in ((w1_ref, m1_ref), (w2_ref, m2_ref)):
        for n in range(2):
            re, im = w[n, 0], w[n, 1]
            m_ref[n, 0:BS, :] = jnp.concatenate([re, im], axis=1)
            m_ref[n, BS:, :] = jnp.concatenate([-im, re], axis=1)
    for copy in wcopies:
        copy.wait()

    @pl.when(me == 0)
    def _():
        w_ref[:, 2 * CO :] = jnp.zeros((3 * CI, CO), BF16)

    @pl.when(me == NLAT - 1)
    def _():
        w_ref[:, :CO] = jnp.zeros((3 * CI, CO), BF16)

    for p in range(ROWS):
        got(0, p, at(p, near, ch))
        if p < LAST:
            go(at(p, near, ch), at(p, far, ch), 3, p, (nxt, ch))
        if p < 2:
            go(at(p, near, ch), at(p, 1, ch), 2, p, (pair, ch2))
        got(1, p, at(p, near, ch2))
        if p < LAST:
            go(at(p, near, ch2), at(p, far, ch2), 4, p, (nxt, ch))
        if p >= 2:
            go(at(p, near, ch2), at(p, 1, ch2), 2, p, (pair, ch))
        if p == 0:
            got(11, LAST, relay_ref)
            go(relay_ref, at(LAST, near, ch), 3, LAST, (pair, ch))
            go(relay_ref, at(LAST, near, ch), 4, LAST, (pair, ch2))
        go(at(p, near, ch), at(p, near, ch), 6, p, (me, core))
        go(at(p, near, ch2), at(p, near, ch2), 7, p, (me, core))

    def conv_row(p, carry):
        got(2, p, at(p, 1, ch2))
        go(at(p, 1, ch2), at(p, 1, ch2), 8, p, (me, core))
        got(3, p, at(p, far, ch))
        go(at(p, far, ch), at(p, far, ch), 9, p, (me, core))
        got(4, p, at(p, far, ch2))
        go(at(p, far, ch2), at(p, far, ch2), 10, p, (me, core))
        got(5, p, at(p, 1, core))
        got(6, p, at(p, near, core))
        got(7, p, at(p, near, core2))
        got(8, p, at(p, 1, core2))
        got(9, p, at(p, far, core))
        got(10, p, at(p, far, core2))
        g = g_ref[p].reshape(3 * CO, PAD)
        for b in range(3):
            part_ref[b] = dot(w_ref[b * CI : (b + 1) * CI, :], g)
        total = part_ref[1]
        for b in (0, 2):
            total = total + shifted(part_ref[b], STEP * (b - 1))
        where = pl.ds(pl.multiple_of(p * BS, 16), BS)
        for n in range(2):
            cg_ref[n, where, :] = total[n * BS : (n + 1) * BS]
            hg_ref[n, where, :] = total[n * BS : (n + 1) * BS].astype(BF16)
        return carry

    lax.fori_loop(0, ROWS, conv_row, 0)

    there = Swap(me, a_ref, r_ref, asend, arecv)
    load(1).wait()
    pl.semaphore_wait(ready, 7)

    def plane(j):
        half = (j + 1) // 2
        return lax.rem(zed + 4 + half - 2 * half * lax.rem(j, 2), 8)

    def analyse(t, carry):
        n, z = t // 8, plane(lax.rem(t, 8))
        where = pl.ds(pl.multiple_of(z * 128, 128), 128)
        block = dot(ana_ref[where, :], hg_ref[n], NT).astype(BF16)
        a_ref[n, pl.ds(z * 8, 8)] = block.reshape(8, 16, PS)
        there.start(n, z)
        return carry

    lax.fori_loop(0, 8, analyse, 0)

    load(0).wait()
    acc_ref[...] = jnp.zeros_like(acc_ref)
    blank2 = jnp.zeros((CI, PAD - LON), F32)

    def kernel_row(p, carry):
        g = g_ref[p].reshape(3 * CO, PAD)
        x = jnp.concatenate([ci_ref[p].astype(F32), blank2], axis=1)
        for b in range(3):
            cib_ref[b * CI : (b + 1) * CI, :] = shifted(x, -STEP * (b - 1)).astype(BF16)
        for b in range(3):
            acc_ref[b * CI : (b + 1) * CI, :] += dot(cib_ref[b * CI : (b + 1) * CI, :], g, NT)
        return carry

    lax.fori_loop(0, ROWS, kernel_row, 0)

    @pl.when(me == 0)
    def _():
        acc_ref[:, 2 * CO :] = jnp.zeros((3 * CI, CO), F32)

    @pl.when(me == NLAT - 1)
    def _():
        acc_ref[:, :CO] = jnp.zeros((3 * CI, CO), F32)

    for rr in range(4):
        for cc in range(2):
            for t in range(3):
                col = cc * 384 + t * 128
                qc_ref[rr * 2 + cc, t * 144 : (t + 1) * 144, :] = acc_ref[
                    rr * 144 : (rr + 1) * 144, col : col + 128
                ].astype(BF16)
    sumc = Summing(me, qc_ref, c1_ref, c2_ref, c3_ref, c4_ref, sumc_ref, csend, crecv)
    sumf = Summing(me, qf_ref, f1_ref, f2_ref, f3_ref, f4_ref, sumf_ref, fsend, frecv)
    sumc.start(0)
    lax.fori_loop(8, 16, analyse, 0)

    home = Swap(me, b_ref, r2_ref, bsend, brecv)
    load(2).wait()
    load(3).wait()
    qf_ref[...] = jnp.zeros_like(qf_ref)

    for copy in ucopies:
        copy.wait()

    def saved(i, carry):
        n, k = i // NK, lax.rem(i, NK)
        here = pl.ds(pl.multiple_of(k * 256, 256), 256)
        b1 = b1_ref[n].astype(F32)
        b1 = jnp.concatenate([b1[0:1], b1[1:2]], axis=1)
        pre = dot(u_ref[n, :, here], m1_ref[n], TN) + b1
        sq = pre * pre
        th = jnp.tanh(ROOT * pre * (1.0 + 0.044715 * sq))
        act_ref[n, :, here] = jnp.transpose(0.5 * pre * (1.0 + th)).astype(BF16)
        slope_ref[n, here, :] = 0.5 * (1.0 + th) + 0.5 * pre * (1.0 - th * th) * (
            ROOT * (1.0 + 3.0 * 0.044715 * sq)
        )
        return carry

    def block_filter(n, carry):
        lax.fori_loop(n * NK, n * NK + NK, saved, 0)

        @pl.when(n == 0)
        def _():
            sumc.wait(0)
            sumc.start(1)

        there.wait_recv(n)
        for half in range(2):
            at_k = slice(half * 448, (half + 1) * 448)
            z_ref[at_k, :] = dot(fwd_ref[at_k, :], r_ref[n].reshape(16 * NLAT, PS))

        def radix(k, carry2):
            top = pl.multiple_of(k * 2 * NLAT, 2 * NLAT)
            zr, zi = z_ref[pl.ds(top, NLAT), :], z_ref[pl.ds(top + NLAT, NLAT), :]
            c, s = tw_ref[0], tw_ref[1]
            zr, zi = zr * c + zi * s, zi * c - zr * s
            wr = [zr[:, p * BS : (p + 1) * BS] for p in range(ROWS)]
            wi = [zi[:, p * BS : (p + 1) * BS] for p in range(ROWS)]
            ar, ai = wr[0] + wr[2], wi[0] + wi[2]
            br, bi = wr[0] - wr[2], wi[0] - wi[2]
            cr, ci = wr[1] + wr[3], wi[1] + wi[3]
            dr, di = wr[1] - wr[3], wi[1] - wi[3]
            vr = jnp.concatenate([ar + cr, br + di, ar - cr, br - di], axis=0)
            vi = jnp.concatenate([ai + ci, bi - dr, ai - ci, bi + dr], axis=0)
            here = pl.ds(pl.multiple_of(k * 256, 256), 256)
            v_ref[here, :] = jnp.concatenate([vr, vi], axis=1).astype(BF16)
            return carry2

        lax.fori_loop(0, NK, radix, 0, unroll=True)
        d_ref[...] = (dot(v_ref[...], m2_ref[n], NT) * slope_ref[n]).astype(BF16)
        x_ref[...] = dot(d_ref[...], m1_ref[n], NT).astype(BF16).astype(F32)

        def unradix(k, carry2):
            top = pl.multiple_of(k * 2 * NLAT, 2 * NLAT)
            c, s = tw_ref[0], tw_ref[1]
            x = x_ref[pl.ds(pl.multiple_of(k * 256, 256), 256), :]
            xr = [x[j * NLAT : (j + 1) * NLAT, :BS] for j in range(4)]
            xi = [x[j * NLAT : (j + 1) * NLAT, BS:] for j in range(4)]
            ar, ai = xr[0] + xr[2], xi[0] + xi[2]
            br, bi = xr[0] - xr[2], xi[0] - xi[2]
            cr, ci = xr[1] + xr[3], xi[1] + xi[3]
            dr, di = xr[1] - xr[3], xi[1] - xi[3]
            er = jnp.concatenate([ar + cr, br - di, ar - cr, br + di], axis=1)
            ei = jnp.concatenate([ai + ci, bi + dr, ai - ci, bi - dr], axis=1)
            e_ref[pl.ds(top, NLAT), :] = (er * c - ei * s).astype(BF16)
            e_ref[pl.ds(top + NLAT, NLAT), :] = (ei * c + er * s).astype(BF16)
            return carry2

        lax.fori_loop(0, NK, unradix, 0, unroll=True)

        g1_ref[...] = dot(u_ref[n], d_ref[...])
        g2_ref[...] = dot(act_ref[n], v_ref[...])
        bias_ref[0:1, :] = jnp.sum(d_ref[...].astype(F32), axis=0, keepdims=True)
        bias_ref[1:2, :] = jnp.sum(v_ref[...].astype(F32), axis=0, keepdims=True)
        for w, (grad, row) in enumerate(((g1_ref, 0), (g2_ref, 1))):
            full = grad[...]
            halves = (full[:BS, :BS] + full[BS:, BS:], full[:BS, BS:] - full[BS:, :BS])
            for part in range(2):
                j = w * 4 + n * 2 + part
                qf_ref[j, 0:BS, 0:BS] = halves[part].astype(BF16)
                tail = bias_ref[row : row + 1, part * BS : (part + 1) * BS]
                qf_ref[j, BS:QF, 0:BS] = jnp.broadcast_to(tail, (QF - BS, BS)).astype(BF16)

        @pl.when(n == 1)
        def _():
            sumf.start(0)

        def inverse(j, carry2):
            z = plane(j)
            where = pl.ds(pl.multiple_of(z * 128, 128), 128)
            block = dot(inv_ref[where, :], e_ref[...]).astype(BF16)
            b_ref[n, pl.ds(z * 8, 8)] = block.reshape(8, 16, PS)
            home.start(n, z)
            return carry2

        lax.fori_loop(0, 2, inverse, 0)

        @pl.when(n == 0)
        def _():
            sumc.wait(1)
            sumc.start(2)

        @pl.when(n == 1)
        def _():
            sumc.wait(2)
            sumc.start(3)
            sumf.wait(0)
            sumf.start(1)

        lax.fori_loop(2, 4, inverse, 0)

        @pl.when(n == 1)
        def _():
            sumf.wait(1)
            sumf.start(2)

        lax.fori_loop(4, 8, inverse, 0)
        return carry

    lax.fori_loop(0, 2, block_filter, 0)
    sumf.wait(2)
    sumf.start(3)
    load(4).wait()

    def synthesis(n):
        home.wait_recv(n)
        for m in range(3):
            lanes = slice(m * 128, (m + 1) * 128)
            modes = r2_ref[n].reshape(16 * NLAT, PS)[:, lanes]
            part = (dot(modes, syn_ref[...], TN) + cg_ref[n, lanes, :])[:, :LON].astype(BF16)
            r = 0
            while r < 128:
                p, s = divmod(m * 128 + r, BS)
                size = min(BS - s, 128 - r)
                out_ref[p, n * BS + s : n * BS + s + size, :] = part[r : r + size]
                r += size

    synthesis(0)
    synthesis(1)
    sumc.wait(3)
    sumf.wait(3)
    for n in range(2):
        there.wait_send(n)
        home.wait_send(n)

    def gather_sent(p, carry):
        for kind in range(11):
            hop(at(p, 1, ch), at(p, 1, ch), kind, p, (me, core)).wait_send()
        return carry

    lax.fori_loop(0, ROWS, gather_sent, 0)
    hop(relay_ref, relay_ref, 11, LAST, (me, core)).wait_send()


def fused(*args):
    vmem, anywhere = pl.BlockSpec(memory_space=pltpu.VMEM), pl.BlockSpec(memory_space=pl.ANY)
    dma = pltpu.SemaphoreType.DMA
    half, wide = BF16, F32
    scratch = [
        ((ROWS, 3, CO, PAD), half), ((ROWS, CI, LON), half), ((3 * CI, 3 * CO), half),
        ((2, CI, NK * 256), half), ((16 * NLAT, PAD), half), ((16 * NLAT, PAD), half),
        ((NK * 2 * NLAT, 16 * NLAT), half), ((16 * NLAT, NK * 2 * NLAT), half),
        ((2, CI, CI), half), ((2, CI, CI), half),
        ((2, PS, PAD), wide), ((2, PS, PAD), half), ((3 * CI, 3 * CO), wide), ((3 * CI, PAD), half),
        ((2, NLAT, 16, PS), half), ((2, NLAT, 16, PS), half), ((2, NLAT, 16, PS), half),
        ((2, NLAT, 16, PS), half), ((NK * 2 * NLAT, PS), wide), ((NK * 2 * NLAT, PS), half),
        ((CI, CI), wide), ((CI, CI), wide), ((8, CI), wide), ((3, CI, PAD), wide),
        ((64, PAD), half), ((2, CI, NK * 256), half), ((2, NK * 256, CI), wide),
        ((NK * 256, CI), half), ((NK * 256, CI), half), ((NK * 256, CI), wide),
        ((8, QC, 128), half), ((8, QF, 128), half),
        ((8, QC, 128), half), ((8 * QCZ, 128), half), ((8, QCZ, 128), half), ((8 * QCZ, 128), half),
        ((8, QF, 128), half), ((8 * QFZ, 128), half), ((8, QFZ, 128), half), ((8 * QFZ, 128), half),
    ]
    return pl.pallas_call(
        fused_kernel,
        out_shape=[
            jax.ShapeDtypeStruct((ROWS, CI, LON), BF16),
            jax.ShapeDtypeStruct((8, QC, 128), BF16),
            jax.ShapeDtypeStruct((8, QF, 128), BF16),
        ],
        in_specs=[vmem] + [anywhere] * 3 + [vmem] * 4 + [anywhere] * 4,
        out_specs=[vmem] * 3,
        scratch_shapes=[pltpu.VMEM(s, t) for s, t in scratch]
        + [
            pltpu.SemaphoreType.REGULAR, dma((5,)), dma((9,)), dma((2 * NK,)), dma((12, ROWS)), dma((12, ROWS)),
            dma((2, NLAT)), dma((2, NLAT)), dma((2, NLAT)), dma((2, NLAT)),
            dma((4, 8)), dma((4, 8)), dma((4, 8)), dma((4, 8)),
        ],
        compiler_params=pltpu.CompilerParams(
            collective_id=0, has_side_effects=True, vmem_limit_bytes=VMEM
        ),
        cost_estimate=pl.CostEstimate(flops=16_000_000_000, bytes_accessed=32 << 20, transcendentals=0),
        name="block_backward",
    )(*args)


def unpack_kernel(in_ref, c_ref, f_ref, out_ref, gc_ref, w1_ref, b1_ref, w2_ref, b2_ref):
    out_ref[...] = in_ref[...]
    for rr in range(4):
        for cc in range(2):
            for t in range(3):
                a, o = divmod(cc * 384 + t * 128, CO)
                r = rr * 144
                while r < (rr + 1) * 144:
                    b, c = divmod(r, CI)
                    n = min(CI - c, (rr + 1) * 144 - r)
                    at = t * 144 + r - rr * 144
                    gc_ref[a, b, c : c + n, o : o + 128] = c_ref[rr * 2 + cc, at : at + n, :].astype(F32)
                    r += n
    for w, (w_ref, b_ref) in enumerate(((w1_ref, b1_ref), (w2_ref, b2_ref))):
        for n in range(2):
            for part in range(2):
                block = f_ref[w * 4 + n * 2 + part].astype(F32)
                w_ref[n, part] = block[:BS, :BS]
                b_ref[n, part : part + 1, :] = block[BS : BS + 1, :BS]


def unpack(grad_in, sumc, sumf):
    vmem = pl.BlockSpec(memory_space=pltpu.VMEM)
    outs = [(3, 3, CI, CO), (2, 2, BS, BS), (2, 2, BS), (2, 2, BS, BS), (2, 2, BS)]
    return pl.pallas_call(
        unpack_kernel,
        out_shape=[jax.ShapeDtypeStruct((ROWS, CI, LON), BF16)]
        + [jax.ShapeDtypeStruct(s, F32) for s in outs],
        in_specs=[vmem] * 3,
        out_specs=[vmem] * 6,
        compiler_params=pltpu.CompilerParams(vmem_limit_bytes=VMEM),
        name="lay_out",
    )(grad_in, sumc, sumf)


def on_device(output_gradient, conv_in, conv_weight, modes, w1, b1, w2):
    ana, syn = lon_tables()
    fwd, inv, tw = lat_tables()
    fwd = fwd.reshape(NK * 2 * NLAT, 16 * NLAT)
    grad_in, sumc, sumf = fused(
        jnp.transpose(output_gradient, (0, 2, 1)),
        jnp.transpose(conv_in, (0, 2, 1)),
        conv_weight,
        jnp.transpose(modes, (0, 2, 3, 4, 1)).reshape(NK, 2, CI, 256),
        w1, b1, w2, tw, ana, syn, fwd, inv,
    )
    grad_in, *sums = unpack(grad_in, sumc, sumf)
    return (jnp.transpose(grad_in, (0, 2, 1)), *sums)


def solution(mesh):
    placed = (
        P("lat", None, "ch"),
        P("lat", None, "ch"),
        P(None, None, "ch", None),
        P("lat", None, "ch", None, None),
        P("ch", None, None, None),
        P("ch", None, None),
        P("ch", None, None, None),
    )
    return jax.shard_map(
        on_device,
        mesh=mesh,
        in_specs=placed,
        out_specs=(
            P("lat", None, "ch"),
            P(None, None, "ch", None),
            P("ch", None, None, None),
            P("ch", None, None),
            P("ch", None, None, None),
            P("ch", None, None),
        ),
        check_vma=False,
    )
```

```python
import functools
import math

import jax
import jax.numpy as jnp
import ml_dtypes
import numpy as np
from jax import lax
from jax.experimental import pallas as pl
from jax.experimental.pallas import tpu as pltpu
from jax.sharding import PartitionSpec as P

MESH = pl.DeviceIdType.MESH
F32, BF16 = jnp.float32, jnp.bfloat16
STEP = 4
LON, PAD = 900, 1024
NLAT = 64
ROWS = 4
NK = 7
KX = 448
CI, CO = 192, 256
BS = 96
PS = ROWS * BS
VMEM = 56 * 1024 * 1024
NT = (((1,), (1,)), ((), ()))
TN = (((0,), (0,)), ((), ()))
NN = (((1,), (0,)), ((), ()))


def dot(a, b, dims=NN):
    return lax.dot_general(a, b, dims, preferred_element_type=F32)


def lon_tables():
    q = np.arange(LON)[None, :]
    d, i, kk = np.meshgrid(np.arange(NLAT), np.arange(2), np.arange(8), indexing="ij")
    k = (d * NK + kk).reshape(-1, 1)
    i = i.reshape(-1, 1)
    live = (kk.reshape(-1, 1) < NK).astype(np.float64)
    angle = (k * q % LON) * (2.0 * math.pi / LON)
    base = np.where(i == 0, np.cos(angle), -np.sin(angle)) / math.sqrt(LON) * live
    weight = np.where(k == 0, 1.0, 2.0)
    pad = ((0, 0), (0, PAD - LON))
    ana = np.pad(base * weight, pad).astype(ml_dtypes.bfloat16)
    syn = np.pad(base, pad).astype(ml_dtypes.bfloat16)
    return ana, syn


def lat_tables():
    y = np.arange(NLAT)[:, None]
    l = np.arange(NLAT)[None, :]
    angle = (y * l % NLAT) * (2.0 * math.pi / NLAT)
    c, s = np.cos(angle) / 16.0, np.sin(angle) / 16.0
    small = np.array([[c, s], [-s, c]])
    fwd = np.zeros((NK, 2, NLAT, NLAT, 2, 8))
    for k in range(NK):
        fwd[k, :, :, :, :, k] = small.transpose(0, 2, 3, 1)
    fwd = fwd.reshape(NK, 2 * NLAT, 16 * NLAT)
    back = np.array([[c, -s], [s, c]])
    inv = np.zeros((NLAT, 2, 8, NK, 2, NLAT))
    for k in range(NK):
        inv[:, :, k, k] = back.transpose(3, 0, 1, 2)
    inv = inv.reshape(16 * NLAT, NK * 2 * NLAT)
    tw = np.zeros((2, ROWS, NLAT, 1))
    for p in range(ROWS):
        a = np.arange(NLAT) * p * (2.0 * math.pi / 256)
        tw[0, p, :, 0], tw[1, p, :, 0] = np.cos(a), np.sin(a)
    tw = np.repeat(tw[..., 0].transpose(0, 2, 1), BS, axis=2)
    return (
        fwd.astype(ml_dtypes.bfloat16),
        inv.astype(ml_dtypes.bfloat16),
        np.ascontiguousarray(tw).astype(np.float32),
    )


def shifted(x, s):
    if s == 0:
        return x
    lane = lax.broadcasted_iota(jnp.int32, x.shape, 1)
    if s > 0:
        return jnp.where(lane < s, pltpu.roll(x, PAD - LON + s, 1), pltpu.roll(x, s, 1))
    return jnp.where(lane >= LON + s, pltpu.roll(x, LON + s, 1), pltpu.roll(x, PAD + s, 1))


class Summing:
    def __init__(self, me, parts, in1, buf2, in2, buf4, out, send, recv):
        self.z, self.spot = me // 8, lax.rem(me, 8)
        self.parts, self.in1, self.buf2, self.in2 = parts, in1, buf2, in2
        self.buf4, self.out, self.send, self.recv = buf4, out, send, recv
        self.rows, self.slot = parts.shape[1], in2.shape[1]

    def copy(self, stage, o, at):
        z, spot = self.z, self.spot
        to_spot, to_z = lax.rem(spot + o, 8), lax.rem(z + o, 8)
        if stage == 0:
            src, dst, lat = self.parts.at[to_spot], self.in1.at[at], z * 8 + to_spot
        elif stage == 1:
            src, dst, lat = self.buf2.at[self.zrows(to_z), :], self.in2.at[at], to_z * 8 + spot
        elif stage == 2:
            src, dst = self.buf4.at[self.zrows(z), :], self.buf4.at[self.zrows(at), :]
            lat = to_z * 8 + spot
        else:
            src, dst, lat = self.buf4.at[pl.ds(0, self.rows), :], self.out.at[at], z * 8 + to_spot
        return pltpu.make_async_remote_copy(
            src_ref=src,
            dst_ref=dst,
            send_sem=self.send.at[stage, o],
            recv_sem=self.recv.at[stage, o],
            device_id={"lat": lat},
            device_id_type=MESH,
        )

    def zrows(self, i):
        return pl.ds(pl.multiple_of(i * self.slot, 16), self.slot)

    def start(self, stage):
        at = self.spot if stage in (0, 3) else self.z

        def go(o, carry):
            self.copy(stage, o, at).start()
            return carry

        lax.fori_loop(1, 8, go, 0)
        if stage == 0:
            self.in1[at] = self.parts[at]
        elif stage == 1:
            self.in2[at] = self.buf2[self.zrows(at), :]
        elif stage == 3:
            self.out[at] = self.buf4[0 : self.rows, :]

    def wait(self, stage):
        at = self.spot if stage in (0, 3) else self.z

        def done(o, carry):
            self.copy(stage, o, lax.rem(at - o + 8, 8)).wait()
            return carry

        lax.fori_loop(1, 8, done, 0)
        if stage == 0:
            total = self.in1[0].astype(F32)
            for i in range(1, 8):
                total = total + self.in1[i].astype(F32)
            self.buf2[0 : self.rows, :] = total.astype(BF16)
            rest = 8 * self.slot - self.rows
            self.buf2[self.rows :, :] = jnp.zeros((rest, 128), BF16)
        elif stage == 1:
            total = self.in2[0].astype(F32)
            for i in range(1, 8):
                total = total + self.in2[i].astype(F32)
            self.buf4[self.zrows(at), :] = total.astype(BF16)


class Swap:
    def __init__(self, me, a, r, send, recv):
        self.me, self.a, self.r, self.send, self.recv = me, a, r, send, recv

    def copy(self, n, to, source):
        return pltpu.make_async_remote_copy(
            src_ref=self.a.at[n, to],
            dst_ref=self.r.at[n, source],
            send_sem=self.send.at[n, to],
            recv_sem=self.recv.at[n, source],
            device_id={"lat": to},
            device_id_type=MESH,
        )

    def start(self, n, z):
        def go(i, carry):
            to = z * 8 + i

            @pl.when(to != self.me)
            def _():
                self.copy(n, to, self.me).start()

            return carry

        lax.fori_loop(0, 8, go, 0)

    def wait_recv(self, n):
        self.r[n, self.me] = self.a[n, self.me]

        def done(o, carry):
            other = lax.rem(self.me + o, NLAT)
            self.copy(n, other, other).wait_recv()
            return carry

        lax.fori_loop(1, NLAT, done, 0)

    def wait_send(self, n):
        def done(o, carry):
            other = lax.rem(self.me + o, NLAT)
            self.copy(n, other, other).wait_send()
            return carry

        lax.fori_loop(1, NLAT, done, 0)


ROOT = math.sqrt(2.0 / math.pi)
QC, QCZ, QF, QFZ = 432, 64, 112, 16
LAST = ROWS - 1


def fused_kernel(
    og_ref, ci_hbm, cw_hbm, u_hbm, w1_ref, b1_ref, w2_ref, tw_ref, ana_hbm, syn_hbm, fwd_hbm, inv_hbm,
    out_ref, sumc_ref, sumf_ref,
    g_ref, ci_ref, w_ref, u_ref, ana_ref, syn_ref, fwd_ref, inv_ref, m1_ref, m2_ref,
    cg_ref, hg_ref, acc_ref, cib_ref, a_ref, r_ref, b_ref, r2_ref, z_ref, e_ref,
    g1_ref, g2_ref, bias_ref, part_ref, relay_ref, act_ref, slope_ref, v_ref, d_ref, x_ref,
    qc_ref, qf_ref, c1_ref, c2_ref, c3_ref, c4_ref, f1_ref, f2_ref, f3_ref, f4_ref,
    ready, loads, wloads, uloads, gsend, grecv, asend, arecv, bsend, brecv, csend, crecv, fsend, frecv,
):
    me = lax.axis_index("lat")
    ch = lax.axis_index("ch")
    zed = me // 8
    xlo = lax.rem(me, 2)
    near = 2 * xlo
    far = 2 - near
    pair = me + 1 - 2 * xlo
    ch2 = lax.rem(ch + 2, 4)
    core = ch + 1 - 2 * lax.rem(ch, 2)
    core2 = lax.rem(core + 2, 4)
    nxt = lax.rem(me + 2 - 4 * xlo + NLAT, NLAT)
    prv = lax.rem(me - 2 + 4 * xlo + NLAT, NLAT)

    barrier = pltpu.get_barrier_semaphore()

    spot = lax.rem(me, 8)
    for dev in ((pair, ch), (pair, ch2), (me, core), (nxt, ch), (prv, ch)):
        pl.semaphore_signal(barrier, inc=1, device_id=dev, device_id_type=MESH)

    def hello(o, carry):
        for lat in (zed * 8 + lax.rem(spot + o, 8), lax.rem(zed + o, 8) * 8 + spot):
            pl.semaphore_signal(barrier, inc=1, device_id=(lat, ch), device_id_type=MESH)
        return carry

    lax.fori_loop(1, 8, hello, 0)

    def load(i):
        pairs = (
            (ci_hbm, ci_ref), (ana_hbm, ana_ref),
            (fwd_hbm, fwd_ref), (inv_hbm, inv_ref), (syn_hbm, syn_ref),
        )
        return pltpu.make_async_copy(pairs[i][0], pairs[i][1], loads.at[i])

    wcopies = []
    for a in range(3):
        for b in range(3):
            wcopies.append(
                pltpu.make_async_copy(
                    cw_hbm.at[a, b],
                    w_ref.at[pl.ds(b * CI, CI), pl.ds(a * CO, CO)],
                    wloads.at[a * 3 + b],
                )
            )
    ucopies = []
    for n in range(2):
        for k in range(NK):
            ucopies.append(
                pltpu.make_async_copy(
                    u_hbm.at[k, n], u_ref.at[n, :, pl.ds(k * 256, 256)], uloads.at[n * NK + k]
                )
            )
    def rows(c):
        return pl.ds(pl.multiple_of(c * 64, 64), 64)

    def at(p, slot, c):
        return g_ref.at[p, slot, rows(c), :]

    blank = jnp.zeros((64, PAD - LON), F32)
    for p in range(ROWS):
        g_ref[p, 1, rows(ch), :] = jnp.concatenate(
            [og_ref[p].astype(F32), blank], axis=1
        ).astype(BF16)
    pl.semaphore_wait(barrier, 5 + 14)

    def plane_here(o, carry):
        lat = lax.rem(zed + o, 8) * 8 + spot
        pl.semaphore_signal(ready, inc=1, device_id=(lat, ch), device_id_type=MESH)
        return carry


    started = []

    def hop(src, dst, kind, p, dev):
        return pltpu.make_async_remote_copy(
            src_ref=src,
            dst_ref=dst,
            send_sem=gsend.at[kind, p],
            recv_sem=grecv.at[kind, p],
            device_id=dev,
            device_id_type=MESH,
        )

    def go(src, dst, kind, p, dev):
        copy = hop(src, dst, kind, p, dev)
        copy.start()

    def got(kind, p, dst):
        hop(dst, dst, kind, p, (me, core)).wait_recv()

    for p in range(ROWS):
        go(at(p, 1, ch), at(p, far, ch), 0, p, (pair, ch))
        go(at(p, 1, ch), at(p, far, ch), 1, p, (pair, ch2))
        if p == 0:
            go(at(LAST, 1, ch), relay_ref, 11, LAST, (prv, ch))
    for p in range(ROWS):
        go(at(p, 1, ch), at(p, 1, ch), 5, p, (me, core))

    lax.fori_loop(1, 8, plane_here, 0)
    for copy in wcopies:
        copy.start()
    for copy in ucopies:
        copy.start()
    for i in range(5):
        load(i).start()

    for w, m_ref in ((w1_ref, m1_ref), (w2_ref, m2_ref)):
        for n in range(2):
            re, im = w[n, 0], w[n, 1]
            m_ref[n, 0:BS, :] = jnp.concatenate([re, im], axis=1)
            m_ref[n, BS:, :] = jnp.concatenate([-im, re], axis=1)
    for copy in wcopies:
        copy.wait()

    @pl.when(me == 0)
    def _():
        w_ref[:, 2 * CO :] = jnp.zeros((3 * CI, CO), BF16)

    @pl.when(me == NLAT - 1)
    def _():
        w_ref[:, :CO] = jnp.zeros((3 * CI, CO), BF16)

    for p in range(ROWS):
        got(0, p, at(p, near, ch))
        if p < LAST:
            go(at(p, near, ch), at(p, far, ch), 3, p, (nxt, ch))
        if p < 2:
            go(at(p, near, ch), at(p, 1, ch), 2, p, (pair, ch2))
        got(1, p, at(p, near, ch2))
        if p < LAST:
            go(at(p, near, ch2), at(p, far, ch2), 4, p, (nxt, ch))
        if p >= 2:
            go(at(p, near, ch2), at(p, 1, ch2), 2, p, (pair, ch))
        if p == 0:
            got(11, LAST, relay_ref)
            go(relay_ref, at(LAST, near, ch), 3, LAST, (pair, ch))
            go(relay_ref, at(LAST, near, ch), 4, LAST, (pair, ch2))
        go(at(p, near, ch), at(p, near, ch), 6, p, (me, core))
        go(at(p, near, ch2), at(p, near, ch2), 7, p, (me, core))

    def conv_row(p, carry):
        got(2, p, at(p, 1, ch2))
        go(at(p, 1, ch2), at(p, 1, ch2), 8, p, (me, core))
        got(3, p, at(p, far, ch))
        go(at(p, far, ch), at(p, far, ch), 9, p, (me, core))
        got(4, p, at(p, far, ch2))
        go(at(p, far, ch2), at(p, far, ch2), 10, p, (me, core))
        got(5, p, at(p, 1, core))
        got(6, p, at(p, near, core))
        got(7, p, at(p, near, core2))
        got(8, p, at(p, 1, core2))
        got(9, p, at(p, far, core))
        got(10, p, at(p, far, core2))
        g = g_ref[p].reshape(3 * CO, PAD)
        for b in range(3):
            part_ref[b] = dot(w_ref[b * CI : (b + 1) * CI, :], g)
        total = part_ref[1]
        for b in (0, 2):
            total = total + shifted(part_ref[b], STEP * (b - 1))
        where = pl.ds(pl.multiple_of(p * BS, 16), BS)
        for n in range(2):
            cg_ref[n, where, :] = total[n * BS : (n + 1) * BS]
            hg_ref[n, where, :] = total[n * BS : (n + 1) * BS].astype(BF16)
        return carry

    lax.fori_loop(0, ROWS, conv_row, 0)

    there = Swap(me, a_ref, r_ref, asend, arecv)
    load(1).wait()
    pl.semaphore_wait(ready, 7)

    def plane(j):
        half = (j + 1) // 2
        return lax.rem(zed + 4 + half - 2 * half * lax.rem(j, 2), 8)

    def analyse(t, carry):
        n, z = t // 8, plane(lax.rem(t, 8))
        where = pl.ds(pl.multiple_of(z * 128, 128), 128)
        block = dot(ana_ref[where, :], hg_ref[n], NT).astype(BF16)
        a_ref[n, pl.ds(z * 8, 8)] = block.reshape(8, 16, PS)
        there.start(n, z)
        return carry

    lax.fori_loop(0, 8, analyse, 0)

    load(0).wait()
    acc_ref[...] = jnp.zeros_like(acc_ref)
    blank2 = jnp.zeros((CI, PAD - LON), F32)

    def kernel_row(p, carry):
        g = g_ref[p].reshape(3 * CO, PAD)
        x = jnp.concatenate([ci_ref[p].astype(F32), blank2], axis=1)
        for b in range(3):
            cib_ref[b * CI : (b + 1) * CI, :] = shifted(x, -STEP * (b - 1)).astype(BF16)
        for b in range(3):
            acc_ref[b * CI : (b + 1) * CI, :] += dot(cib_ref[b * CI : (b + 1) * CI, :], g, NT)
        return carry

    lax.fori_loop(0, ROWS, kernel_row, 0)

    @pl.when(me == 0)
    def _():
        acc_ref[:, 2 * CO :] = jnp.zeros((3 * CI, CO), F32)

    @pl.when(me == NLAT - 1)
    def _():
        acc_ref[:, :CO] = jnp.zeros((3 * CI, CO), F32)

    for rr in range(4):
        for cc in range(2):
            for t in range(3):
                col = cc * 384 + t * 128
                qc_ref[rr * 2 + cc, t * 144 : (t + 1) * 144, :] = acc_ref[
                    rr * 144 : (rr + 1) * 144, col : col + 128
                ].astype(BF16)
    sumc = Summing(me, qc_ref, c1_ref, c2_ref, c3_ref, c4_ref, sumc_ref, csend, crecv)
    sumf = Summing(me, qf_ref, f1_ref, f2_ref, f3_ref, f4_ref, sumf_ref, fsend, frecv)
    sumc.start(0)
    lax.fori_loop(8, 16, analyse, 0)

    home = Swap(me, b_ref, r2_ref, bsend, brecv)
    load(2).wait()
    load(3).wait()
    qf_ref[...] = jnp.zeros_like(qf_ref)

    for copy in ucopies:
        copy.wait()

    def saved(i, carry):
        n, k = i // NK, lax.rem(i, NK)
        here = pl.ds(pl.multiple_of(k * 256, 256), 256)
        b1 = b1_ref[n].astype(F32)
        b1 = jnp.concatenate([b1[0:1], b1[1:2]], axis=1)
        pre = dot(u_ref[n, :, here], m1_ref[n], TN) + b1
        sq = pre * pre
        th = jnp.tanh(ROOT * pre * (1.0 + 0.044715 * sq))
        act_ref[n, :, here] = jnp.transpose(0.5 * pre * (1.0 + th)).astype(BF16)
        slope_ref[n, here, :] = 0.5 * (1.0 + th) + 0.5 * pre * (1.0 - th * th) * (
            ROOT * (1.0 + 3.0 * 0.044715 * sq)
        )
        return carry

    def block_filter(n, carry):
        lax.fori_loop(n * NK, n * NK + NK, saved, 0)

        @pl.when(n == 0)
        def _():
            sumc.wait(0)
            sumc.start(1)

        there.wait_recv(n)
        for half in range(2):
            at_k = slice(half * 448, (half + 1) * 448)
            z_ref[at_k, :] = dot(fwd_ref[at_k, :], r_ref[n].reshape(16 * NLAT, PS))

        def radix(k, carry2):
            top = pl.multiple_of(k * 2 * NLAT, 2 * NLAT)
            zr, zi = z_ref[pl.ds(top, NLAT), :], z_ref[pl.ds(top + NLAT, NLAT), :]
            c, s = tw_ref[0], tw_ref[1]
            zr, zi = zr * c + zi * s, zi * c - zr * s
            wr = [zr[:, p * BS : (p + 1) * BS] for p in range(ROWS)]
            wi = [zi[:, p * BS : (p + 1) * BS] for p in range(ROWS)]
            ar, ai = wr[0] + wr[2], wi[0] + wi[2]
            br, bi = wr[0] - wr[2], wi[0] - wi[2]
            cr, ci = wr[1] + wr[3], wi[1] + wi[3]
            dr, di = wr[1] - wr[3], wi[1] - wi[3]
            vr = jnp.concatenate([ar + cr, br + di, ar - cr, br - di], axis=0)
            vi = jnp.concatenate([ai + ci, bi - dr, ai - ci, bi + dr], axis=0)
            here = pl.ds(pl.multiple_of(k * 256, 256), 256)
            v_ref[here, :] = jnp.concatenate([vr, vi], axis=1).astype(BF16)
            return carry2

        lax.fori_loop(0, NK, radix, 0, unroll=True)
        d_ref[...] = (dot(v_ref[...], m2_ref[n], NT) * slope_ref[n]).astype(BF16)
        x_ref[...] = dot(d_ref[...], m1_ref[n], NT).astype(BF16).astype(F32)

        def unradix(k, carry2):
            top = pl.multiple_of(k * 2 * NLAT, 2 * NLAT)
            c, s = tw_ref[0], tw_ref[1]
            x = x_ref[pl.ds(pl.multiple_of(k * 256, 256), 256), :]
            xr = [x[j * NLAT : (j + 1) * NLAT, :BS] for j in range(4)]
            xi = [x[j * NLAT : (j + 1) * NLAT, BS:] for j in range(4)]
            ar, ai = xr[0] + xr[2], xi[0] + xi[2]
            br, bi = xr[0] - xr[2], xi[0] - xi[2]
            cr, ci = xr[1] + xr[3], xi[1] + xi[3]
            dr, di = xr[1] - xr[3], xi[1] - xi[3]
            er = jnp.concatenate([ar + cr, br - di, ar - cr, br + di], axis=1)
            ei = jnp.concatenate([ai + ci, bi + dr, ai - ci, bi - dr], axis=1)
            e_ref[pl.ds(top, NLAT), :] = (er * c - ei * s).astype(BF16)
            e_ref[pl.ds(top + NLAT, NLAT), :] = (ei * c + er * s).astype(BF16)
            return carry2

        lax.fori_loop(0, NK, unradix, 0, unroll=True)

        g1_ref[...] = dot(u_ref[n], d_ref[...])
        g2_ref[...] = dot(act_ref[n], v_ref[...])
        bias_ref[0:1, :] = jnp.sum(d_ref[...].astype(F32), axis=0, keepdims=True)
        bias_ref[1:2, :] = jnp.sum(v_ref[...].astype(F32), axis=0, keepdims=True)
        for w, (grad, row) in enumerate(((g1_ref, 0), (g2_ref, 1))):
            full = grad[...]
            halves = (full[:BS, :BS] + full[BS:, BS:], full[:BS, BS:] - full[BS:, :BS])
            for part in range(2):
                j = w * 4 + n * 2 + part
                qf_ref[j, 0:BS, 0:BS] = halves[part].astype(BF16)
                tail = bias_ref[row : row + 1, part * BS : (part + 1) * BS]
                qf_ref[j, BS:QF, 0:BS] = jnp.broadcast_to(tail, (QF - BS, BS)).astype(BF16)

        @pl.when(n == 1)
        def _():
            sumf.start(0)

        def inverse(j, carry2):
            z = plane(j)
            where = pl.ds(pl.multiple_of(z * 128, 128), 128)
            block = dot(inv_ref[where, :], e_ref[...]).astype(BF16)
            b_ref[n, pl.ds(z * 8, 8)] = block.reshape(8, 16, PS)
            home.start(n, z)
            return carry2

        lax.fori_loop(0, 2, inverse, 0)

        @pl.when(n == 0)
        def _():
            sumc.wait(1)
            sumc.start(2)

        @pl.when(n == 1)
        def _():
            sumc.wait(2)
            sumc.start(3)

        lax.fori_loop(2, 4, inverse, 0)

        @pl.when(n == 1)
        def _():
            sumf.wait(0)
            sumf.start(1)

        lax.fori_loop(4, 8, inverse, 0)
        return carry

    lax.fori_loop(0, 2, block_filter, 0)
    load(4).wait()

    def synthesis(n):
        home.wait_recv(n)
        for m in range(3):
            lanes = slice(m * 128, (m + 1) * 128)
            modes = r2_ref[n].reshape(16 * NLAT, PS)[:, lanes]
            part = (dot(modes, syn_ref[...], TN) + cg_ref[n, lanes, :])[:, :LON].astype(BF16)
            r = 0
            while r < 128:
                p, s = divmod(m * 128 + r, BS)
                size = min(BS - s, 128 - r)
                out_ref[p, n * BS + s : n * BS + s + size, :] = part[r : r + size]
                r += size

    sumf.wait(1)
    sumf.start(2)
    synthesis(0)
    sumf.wait(2)
    sumf.start(3)
    synthesis(1)
    sumc.wait(3)
    sumf.wait(3)
    for n in range(2):
        there.wait_send(n)
        home.wait_send(n)

    def gather_sent(p, carry):
        for kind in range(11):
            hop(at(p, 1, ch), at(p, 1, ch), kind, p, (me, core)).wait_send()
        return carry

    lax.fori_loop(0, ROWS, gather_sent, 0)
    hop(relay_ref, relay_ref, 11, LAST, (me, core)).wait_send()


def fused(*args):
    vmem, anywhere = pl.BlockSpec(memory_space=pltpu.VMEM), pl.BlockSpec(memory_space=pl.ANY)
    dma = pltpu.SemaphoreType.DMA
    half, wide = BF16, F32
    scratch = [
        ((ROWS, 3, CO, PAD), half), ((ROWS, CI, LON), half), ((3 * CI, 3 * CO), half),
        ((2, CI, NK * 256), half), ((16 * NLAT, PAD), half), ((16 * NLAT, PAD), half),
        ((NK * 2 * NLAT, 16 * NLAT), half), ((16 * NLAT, NK * 2 * NLAT), half),
        ((2, CI, CI), half), ((2, CI, CI), half),
        ((2, PS, PAD), wide), ((2, PS, PAD), half), ((3 * CI, 3 * CO), wide), ((3 * CI, PAD), half),
        ((2, NLAT, 16, PS), half), ((2, NLAT, 16, PS), half), ((2, NLAT, 16, PS), half),
        ((2, NLAT, 16, PS), half), ((NK * 2 * NLAT, PS), wide), ((NK * 2 * NLAT, PS), half),
        ((CI, CI), wide), ((CI, CI), wide), ((8, CI), wide), ((3, CI, PAD), wide),
        ((64, PAD), half), ((2, CI, NK * 256), half), ((2, NK * 256, CI), wide),
        ((NK * 256, CI), half), ((NK * 256, CI), half), ((NK * 256, CI), wide),
        ((8, QC, 128), half), ((8, QF, 128), half),
        ((8, QC, 128), half), ((8 * QCZ, 128), half), ((8, QCZ, 128), half), ((8 * QCZ, 128), half),
        ((8, QF, 128), half), ((8 * QFZ, 128), half), ((8, QFZ, 128), half), ((8 * QFZ, 128), half),
    ]
    return pl.pallas_call(
        fused_kernel,
        out_shape=[
            jax.ShapeDtypeStruct((ROWS, CI, LON), BF16),
            jax.ShapeDtypeStruct((8, QC, 128), BF16),
            jax.ShapeDtypeStruct((8, QF, 128), BF16),
        ],
        in_specs=[vmem] + [anywhere] * 3 + [vmem] * 4 + [anywhere] * 4,
        out_specs=[vmem] * 3,
        scratch_shapes=[pltpu.VMEM(s, t) for s, t in scratch]
        + [
            pltpu.SemaphoreType.REGULAR, dma((5,)), dma((9,)), dma((2 * NK,)), dma((12, ROWS)), dma((12, ROWS)),
            dma((2, NLAT)), dma((2, NLAT)), dma((2, NLAT)), dma((2, NLAT)),
            dma((4, 8)), dma((4, 8)), dma((4, 8)), dma((4, 8)),
        ],
        compiler_params=pltpu.CompilerParams(
            collective_id=0, has_side_effects=True, vmem_limit_bytes=VMEM
        ),
        cost_estimate=pl.CostEstimate(flops=16_000_000_000, bytes_accessed=32 << 20, transcendentals=0),
        name="block_backward",
    )(*args)


def unpack_kernel(
    in_hbm, c_ref, f_ref, out_hbm, gc_ref, w1_ref, b1_ref, w2_ref, b2_ref, rows_ref, taken, given
):
    take = [
        pltpu.make_async_copy(in_hbm.at[p], rows_ref.at[p], taken.at[p]) for p in range(ROWS)
    ]
    give = [
        pltpu.make_async_copy(rows_ref.at[p], out_hbm.at[p], given.at[p]) for p in range(ROWS)
    ]
    for move in take:
        move.start()
    for rr in range(4):
        for cc in range(2):
            for t in range(3):
                a, o = divmod(cc * 384 + t * 128, CO)
                r = rr * 144
                while r < (rr + 1) * 144:
                    b, c = divmod(r, CI)
                    n = min(CI - c, (rr + 1) * 144 - r)
                    at = t * 144 + r - rr * 144
                    gc_ref[a, b, c : c + n, o : o + 128] = c_ref[rr * 2 + cc, at : at + n, :].astype(F32)
                    r += n
    for p in range(ROWS):
        take[p].wait()
        give[p].start()
    for w, (w_ref, b_ref) in enumerate(((w1_ref, b1_ref), (w2_ref, b2_ref))):
        for n in range(2):
            for part in range(2):
                block = f_ref[w * 4 + n * 2 + part].astype(F32)
                w_ref[n, part] = block[:BS, :BS]
                b_ref[n, part : part + 1, :] = block[BS : BS + 1, :BS]
    for move in give:
        move.wait()


def unpack(grad_in, sumc, sumf):
    vmem, anywhere = pl.BlockSpec(memory_space=pltpu.VMEM), pl.BlockSpec(memory_space=pl.ANY)
    outs = [(3, 3, CI, CO), (2, 2, BS, BS), (2, 2, BS), (2, 2, BS, BS), (2, 2, BS)]
    return pl.pallas_call(
        unpack_kernel,
        out_shape=[jax.ShapeDtypeStruct((ROWS, CI, LON), BF16)]
        + [jax.ShapeDtypeStruct(s, F32) for s in outs],
        in_specs=[anywhere] + [vmem] * 2,
        out_specs=[anywhere] + [vmem] * 5,
        scratch_shapes=[
            pltpu.VMEM((ROWS, CI, LON), BF16),
            pltpu.SemaphoreType.DMA((ROWS,)),
            pltpu.SemaphoreType.DMA((ROWS,)),
        ],
        compiler_params=pltpu.CompilerParams(vmem_limit_bytes=VMEM),
        name="lay_out",
    )(grad_in, sumc, sumf)


def on_device(output_gradient, conv_in, conv_weight, modes, w1, b1, w2):
    ana, syn = lon_tables()
    fwd, inv, tw = lat_tables()
    fwd = fwd.reshape(NK * 2 * NLAT, 16 * NLAT)
    grad_in, sumc, sumf = fused(
        jnp.transpose(output_gradient, (0, 2, 1)),
        jnp.transpose(conv_in, (0, 2, 1)),
        conv_weight,
        jnp.transpose(modes, (0, 2, 3, 4, 1)).reshape(NK, 2, CI, 256),
        w1, b1, w2, tw, ana, syn, fwd, inv,
    )
    grad_in, *sums = unpack(grad_in, sumc, sumf)
    return (jnp.transpose(grad_in, (0, 2, 1)), *sums)


def solution(mesh):
    placed = (
        P("lat", None, "ch"),
        P("lat", None, "ch"),
        P(None, None, "ch", None),
        P("lat", None, "ch", None, None),
        P("ch", None, None, None),
        P("ch", None, None),
        P("ch", None, None, None),
    )
    return jax.shard_map(
        on_device,
        mesh=mesh,
        in_specs=placed,
        out_specs=(
            P("lat", None, "ch"),
            P(None, None, "ch", None),
            P("ch", None, None, None),
            P("ch", None, None),
            P("ch", None, None, None),
            P("ch", None, None),
        ),
        check_vma=False,
    )
```
